128 devices in a mesh: kvseq: 16 (over z, x), kvhead: 8 (over y, core).
Axes of the slice: x: 4, y: 4, z: 4, core: 2. Of those that a mesh axis runs over, the one named last changes fastest.
Arguments:
- hidden_in: bfloat16 [16, 16384], P(None, 'kvseq'), may hold values from -8 to 8
- queries: bfloat16 [4, 4, 64, 128], P(None, None, 'kvhead'), may hold values from -110 to 110
- new_keys: bfloat16 [4, 4, 8, 128], P(None, None, 'kvhead'), may hold values from -4 to 4
- new_values: bfloat16 [4, 4, 8, 128], P(None, None, 'kvhead'), may hold values from -12 to 12
- cache_keys: bfloat16 [4, 16384, 8, 128], P(None, 'kvseq', 'kvhead'), may hold values from -4 to 4
- cache_values: bfloat16 [4, 16384, 8, 128], P(None, 'kvseq', 'kvhead'), may hold values from -12 to 12
- lengths: int32 [4], replicated, may hold values from 128 to 16384, as said below
- out_weight: bfloat16 [8192, 16384], P('kvhead', 'kvseq'), may hold values from -0.5 to 0.5
- norm_gain: float32 [16384], P('kvseq'), may hold values from 0.1 to 1.9
- gate_weight: bfloat16 [16384, 26624], P('kvseq', 'kvhead'), may hold values from -0.046875 to 0.046875
- up_weight: bfloat16 [16384, 26624], P('kvseq', 'kvhead'), may hold values from -0.046875 to 0.046875
- down_weight: bfloat16 [26624, 16384], P('kvhead', 'kvseq'), may hold values from -0.0390625 to 0.0390625
Outputs:
- layer_out: bfloat16 [16, 16384], P('kvhead', 'kvseq')
The draws below stay inside these ranges and needn't reach their ends.
Inputs may be any that keep to these rules, and one draw needn't show every extreme that they name: `lengths`: each length is a multiple of 128; some request has exactly 16384.
All inputs are finite; a program needn't handle non-finite values.
Results may differ from the reference program's by a relative error of at most 0.01.
Values may be sent and summed in bfloat16 or wider, within the bound.
No kernel may reach another device: no remote copies, remote signals or barrier semaphores. Data moves between devices by JAX's collectives and lax.ppermute only.
A program may use at most 64 MiB of HBM per device.

```python
import math
import jax
import jax.numpy as jnp
from jax import lax

D = 16384
QH = 64
KVH = 8
HD = 128
FF = 26624
REQS = 4
STEPS = 4
TOK = 16
CTX = 16384


def shared_keys(key):
    return jnp.clip(jax.random.normal(jax.random.fold_in(key, 101), (REQS, CTX, KVH, HD), jnp.float32), -4.0, 4.0)


def draw_cache_keys(key, part):
    base = shared_keys(key)
    return base.astype(jnp.bfloat16)


def draw_queries(key, part):
    key = jax.random.fold_in(key, 2)
    values = jnp.clip(jax.random.normal(key, (REQS, STEPS, QH, HD), jnp.float32), -4.0, 4.0)
    return values.astype(jnp.bfloat16)


def draw_hidden_in(key, part):
    key = jax.random.fold_in(key, 1)
    column = jnp.arange(D).astype(jnp.float32) / D
    base = jnp.clip(jax.random.normal(key, (TOK, D), jnp.float32), -4.0, 4.0) * (0.6 + 1.2 * column)[None, :]
    return base.astype(jnp.bfloat16)


def draw_lengths(key, part):
    key = jax.random.fold_in(key, 4)
    blocks = jax.random.randint(key, (REQS,), 1, CTX // 128 + 1)
    longest = jax.random.randint(jax.random.fold_in(key, 5), (), 0, REQS)
    blocks = jnp.where(jnp.arange(REQS) == longest, CTX // 128, blocks)
    return (blocks * 128).astype(jnp.int32)


def shard_levels(own_key, shape, cuts, least, top_value):
    factor_of, own = 1.0, jax.random.fold_in(own_key, 6)
    for axis_at, shards_of in cuts:
        steps = jnp.exp(jax.random.uniform(jax.random.fold_in(own, axis_at), (shards_of,), jnp.float32, least / len(cuts), top_value / len(cuts)))
        factor_of = factor_of * jnp.repeat(steps, shape[axis_at] // shards_of).reshape([-1 if axis == axis_at else 1 for axis in range(len(shape))])
    return factor_of


def bell_draw(key, shape, scale, reach, shards=(), held_as=jnp.bfloat16):
    factor_of = shard_levels(key, shape, shards, -0.22, 0.18) if shards else 1.0
    values = jax.random.normal(key, shape, jnp.float32) * scale * factor_of
    return jnp.minimum(jnp.maximum(values, -reach), reach).astype(held_as)


def setup_inputs(seed: int = 0) -> dict:
    keys = jax.random.split(jax.random.key(seed), 13)
    hidden_in = draw_hidden_in(jax.random.fold_in(keys[12], 71), 0)
    queries = draw_queries(jax.random.fold_in(keys[12], 71), 0)
    new_keys = bell_draw(keys[2], (REQS, STEPS, KVH, HD), 1.0, 4.0, ((2, 8),))
    new_values = bell_draw(keys[3], (REQS, STEPS, KVH, HD), 3.0, 12.0, ((2, 8),))
    cache_keys = draw_cache_keys(jax.random.fold_in(keys[12], 71), 0)
    cache_values = bell_draw(keys[5], (REQS, CTX, KVH, HD), 3.0, 12.0, ((1, 16), (2, 8)))
    lengths = draw_lengths(jax.random.fold_in(keys[12], 71), 0)
    out_weight = bell_draw(keys[7], (QH * HD, D), HD ** -0.5, 0.5, ((0, 8), (1, 16)))
    norm_gain = jnp.clip(1.0 + 0.18 * jax.random.normal(keys[8], (D,), jnp.float32), 0.1, 1.9)
    gate_weight = bell_draw(keys[9], (D, FF), D ** -0.5, 0.046875, ((0, 16), (1, 8)))
    up_weight = bell_draw(keys[10], (D, FF), D ** -0.5, 0.046875, ((0, 16), (1, 8)))
    down_weight = bell_draw(keys[11], (FF, D), FF ** -0.5, 0.0390625, ((0, 8), (1, 16)))
    return dict(hidden_in=hidden_in, queries=queries, new_keys=new_keys, new_values=new_values, cache_keys=cache_keys, cache_values=cache_values, lengths=lengths, out_weight=out_weight, norm_gain=norm_gain, gate_weight=gate_weight, up_weight=up_weight, down_weight=down_weight)


MASKED = -1e+30

def reference(hidden_in, queries, new_keys, new_values, cache_keys, cache_values, lengths, out_weight, norm_gain, gate_weight, up_weight, down_weight):
    score_scale = 1.0 / math.sqrt(HD)
    query_all = queries.astype(jnp.float32).reshape(REQS, STEPS, KVH, QH // KVH, HD)
    cache_scores = jnp.einsum('rskgd,rckd->rskgc', query_all, cache_keys.astype(jnp.float32)) * score_scale
    fresh_scores = jnp.einsum('rskgd,rtkd->rskgt', query_all, new_keys.astype(jnp.float32)) * score_scale
    cache_mask = (jnp.arange(CTX)[None, :] < lengths[:, None])[:, None, None, None, :]
    step_ids = jnp.arange(STEPS)
    fresh_mask = (step_ids[None, :] <= step_ids[:, None])[None, :, None, None, :]
    row_max = jnp.maximum(lax.optimization_barrier(jnp.max(jnp.where(cache_mask, cache_scores, MASKED), axis=-1)), lax.optimization_barrier(jnp.max(jnp.where(fresh_mask, fresh_scores, MASKED), axis=-1)))
    cache_prob = jnp.where(cache_mask, jnp.exp(cache_scores - row_max[..., None]), 0.0)
    fresh_prob = jnp.where(fresh_mask, jnp.exp(fresh_scores - row_max[..., None]), 0.0)
    row_total = lax.optimization_barrier(jnp.sum(cache_prob, axis=-1)) + lax.optimization_barrier(jnp.sum(fresh_prob, axis=-1))
    weighted = jnp.einsum('rskgc,rckd->rskgd', cache_prob, cache_values.astype(jnp.float32))
    weighted = weighted + jnp.einsum('rskgt,rtkd->rskgd', fresh_prob, new_values.astype(jnp.float32))
    attended = (weighted / row_total[..., None]).reshape(TOK, QH * HD).astype(jnp.bfloat16)
    residual = hidden_in.astype(jnp.float32) + jnp.dot(attended, out_weight, preferred_element_type=jnp.float32)
    mean_square = lax.optimization_barrier(jnp.mean(residual * residual, axis=-1))
    normed = (residual * lax_rsqrt(mean_square + 1e-05)[:, None] * norm_gain[None, :]).astype(jnp.bfloat16)
    gate_total = jnp.dot(normed, gate_weight, preferred_element_type=jnp.float32)
    up_total = jnp.dot(normed, up_weight, preferred_element_type=jnp.float32)
    hidden = (jax.nn.silu(gate_total) * up_total).astype(jnp.bfloat16)
    down_total = jnp.dot(hidden, down_weight, preferred_element_type=jnp.float32)
    return (residual + down_total).astype(jnp.bfloat16)

def lax_rsqrt(value):
    return 1.0 / jnp.sqrt(value)
```

```python
import functools
import math

import jax
import jax.numpy as jnp
from jax import lax
from jax.experimental import pallas as pl
from jax.experimental.pallas import tpu as pltpu
from jax.sharding import PartitionSpec as P

MASKED = -1e30
F32 = jnp.float32
BF16 = jnp.bfloat16
LANES = 128
RING = 4
SHIFTS = (2, 1, 3)


def ring_index(axis, stride):
    return lax.rem(lax.div(lax.axis_index(axis), stride), RING)


def moved(part, axis, stride, shift):
    pairs = []
    for at in range(lax.axis_size(axis)):
        place = (at // stride) % RING
        pairs.append((at, at + ((place + shift) % RING - place) * stride))
    return lax.ppermute(part, axis, pairs)


def from_others(part, axis, stride):
    return [moved(part, axis, stride, shift) for shift in (1, 2, 3)]


def chunks_from_others(chunks, axis, stride):
    return [moved(chunks[shift], axis, stride, shift) for shift in (1, 2, 3)]


def vmem(*arrays):
    return [pltpu.with_memory_space_constraint(array, pltpu.VMEM) for array in arrays]


def whole(count):
    return [pl.BlockSpec(memory_space=pltpu.VMEM)] * count


def kept(shape, dtype):
    return pltpu.VMEM(shape, dtype)


def params(mib):
    return pltpu.CompilerParams(vmem_limit_bytes=mib << 20)


def diagonal(size):
    rows = lax.broadcasted_iota(jnp.int32, (size, size), 0)
    columns = lax.broadcasted_iota(jnp.int32, (size, size), 1)
    return rows == columns


def three_parts(value):
    first = value.astype(BF16)
    rest = value - first.astype(F32)
    second = rest.astype(BF16)
    third = (rest - second.astype(F32)).astype(BF16)
    return first.astype(F32), second.astype(F32), third.astype(F32)


def packed_levels(level, rows):
    size = level.shape[0]
    line = jnp.sum(
        jnp.where(diagonal(size), jnp.broadcast_to(level, (size, size)), 0.0), axis=0, keepdims=True
    )
    row = lax.broadcasted_iota(jnp.int32, (rows, size), 0)
    tile = jnp.zeros((rows, size), F32)
    for at, part in enumerate(three_parts(line)):
        tile = jnp.where(row == at, jnp.broadcast_to(part, (rows, size)), tile)
    return tile.astype(BF16)


def attention_kernel(
    shard_slots, lengths, query, keys, values, fresh_keys, fresh_values, out, level
):
    request = pl.program_id(0)
    shard = lax.axis_index("kvseq")
    rows, head_dim = query.shape[1:]
    steps = fresh_keys.shape[1]
    scale = 1.0 / math.sqrt(head_dim)
    contract = (((1,), (1,)), ((), ()))
    mine = query[0]
    slots = keys.shape[1]
    scores = lax.dot_general(mine, keys[0], contract, preferred_element_type=F32) * scale
    valid = lengths[request] - shard * shard_slots
    mask = lax.broadcasted_iota(jnp.int32, (rows, slots), 1) < valid
    fresh_scores = (
        lax.dot_general(mine, fresh_keys[0], contract, preferred_element_type=F32) * scale
    )
    step = lax.div(lax.broadcasted_iota(jnp.int32, (rows, steps), 0), rows // steps)
    token = lax.broadcasted_iota(jnp.int32, (rows, steps), 1)
    fresh_mask = token <= jnp.where(shard == 0, step, -1)
    scores = jnp.where(mask, scores, MASKED)
    fresh_scores = jnp.where(fresh_mask, fresh_scores, MASKED)
    top = jnp.maximum(
        jnp.max(scores, axis=1, keepdims=True), jnp.max(fresh_scores, axis=1, keepdims=True)
    )
    prob = jnp.where(mask, jnp.exp(scores - top), 0.0)
    fresh_prob = jnp.where(fresh_mask, jnp.exp(fresh_scores - top), 0.0)
    total = jnp.sum(prob, axis=1, keepdims=True) + jnp.sum(fresh_prob, axis=1, keepdims=True)
    weighted = jnp.dot(prob.astype(BF16), values[0], preferred_element_type=F32) + jnp.dot(
        fresh_prob.astype(BF16), fresh_values[0], preferred_element_type=F32
    )
    some = total > 0.0
    safe = jnp.where(some, total, 1.0)
    mean = (weighted / safe).astype(BF16)
    mine_level = jnp.where(some, top + jnp.log(safe), MASKED)
    half = rows // 2
    groups = pl.num_programs(0)
    for part in range(2):
        start = pl.multiple_of(part * half * RING + request * half, half)
        out[pl.ds(start, half), :] = mean[part * half : (part + 1) * half]
        level[pl.ds(start, half), :] = jnp.broadcast_to(
            mine_level[part * half : (part + 1) * half], (half, level.shape[1])
        )

    @pl.when(request == groups - 1)
    def _():
        count = rows * RING
        out[count : count + 16, :] = packed_levels(level[:, :1], 16)


def attention(queries, new_keys, new_values, cache_keys, cache_values, lengths):
    requests, slots, _, head_dim = cache_keys.shape
    rows = queries.shape[1] * queries.shape[2]
    steps = new_keys.shape[1]
    count = requests * rows

    def block(*shape):
        return pl.BlockSpec((1, *shape), lambda r: (r, 0, 0))

    return pl.pallas_call(
        functools.partial(attention_kernel, slots),
        grid=(requests,),
        in_specs=[
            pl.BlockSpec(memory_space=pltpu.SMEM),
            block(rows, head_dim),
            block(slots, head_dim),
            block(slots, head_dim),
            block(steps, head_dim),
            block(steps, head_dim),
        ],
        out_specs=pl.BlockSpec((count + 16, head_dim), lambda r: (0, 0)),
        out_shape=kept((count + 16, head_dim), BF16),
        scratch_shapes=[pltpu.VMEM((count, LANES), F32)],
        compiler_params=params(6),
        name="attention",
    )(
        lengths,
        queries.reshape(requests, rows, head_dim),
        cache_keys.reshape(requests, slots, head_dim),
        cache_values.reshape(requests, slots, head_dim),
        new_keys.reshape(requests, steps, head_dim),
        new_values.reshape(requests, steps, head_dim),
    )


def merge(parts):
    count = parts[0].shape[0] - 16
    same = diagonal(count)
    levels, means = [], []
    for part in parts:
        tail = part[count:, :].astype(F32)
        line = tail[0:1] + tail[1:2] + tail[2:3]
        levels.append(
            jnp.sum(
                jnp.where(same, jnp.broadcast_to(line, (count, count)), 0.0), axis=1, keepdims=True
            )
        )
        means.append(part[:count, :].astype(F32))
    top = functools.reduce(jnp.maximum, levels)
    scales = [jnp.exp(level - top) for level in levels]
    total = sum(scales)
    mean = sum(scale * mean for scale, mean in zip(scales, means)) / total
    return mean, top + jnp.log(total)


def merge_kernel(*refs):
    parts, out = refs[:RING], refs[RING]
    mean, level = merge(parts)
    count = mean.shape[0]
    out[:count, :] = mean.astype(BF16)
    out[count:, :] = packed_levels(level, 16)


def merged(parts):
    return pl.pallas_call(
        merge_kernel,
        in_specs=whole(RING),
        out_specs=whole(1)[0],
        out_shape=kept(parts[0].shape, BF16),
        compiler_params=params(4),
        name="merge_x",
    )(*vmem(*parts))


def project_kernel(*refs):
    parts, weight, out, attended = refs[:RING], refs[RING], refs[RING + 1], refs[RING + 2]
    mean, _ = merge(parts)
    attended[...] = mean
    rows = out.shape[0]
    heads = mean.shape[0] // rows
    row = jnp.concatenate(
        [attended[pl.ds(head, rows, stride=heads), :].astype(BF16) for head in range(heads)], axis=1
    )
    out[...] = jnp.dot(row, weight[...], preferred_element_type=F32)


def projected(parts, weight, rows):
    count, head_dim = parts[0].shape
    return pl.pallas_call(
        project_kernel,
        in_specs=whole(RING + 1),
        out_specs=whole(1)[0],
        out_shape=kept((rows, weight.shape[1]), F32),
        scratch_shapes=[pltpu.VMEM((count - 16, head_dim), F32)],
        compiler_params=params(4),
        name="merge_z_project",
    )(*vmem(*parts, weight))


def up_kernel(width, hidden_in, first, second, third, fourth, gain, gate, up, out, residual):
    place = ring_index("kvseq", 1)
    total = (
        hidden_in[...].astype(F32)
        + first[...].astype(F32)
        + second[...].astype(F32)
        + third[...].astype(F32)
        + fourth[...].astype(F32)
    )
    residual[...] = total
    squares = jnp.sum(total * total, axis=1, keepdims=True)
    high = squares.astype(BF16).astype(F32)
    rows = total.shape[0]
    lane = lax.broadcasted_iota(jnp.int32, (rows, LANES), 1)
    tail = jnp.where(lane < LANES // 2, high, squares - high).astype(BF16)
    scaled = (total * gain[...]).astype(BF16)
    columns = gate.shape[1]
    for part in range(RING):
        start = part * width
        real = min(width, columns - start)
        at = lax.rem(part + RING - place, RING)
        for offset, weight in ((0, gate), (width, up)):
            terms = jnp.dot(scaled, weight[:, start : start + real], preferred_element_type=F32)
            out[at, :, offset : offset + real] = terms.astype(BF16)
            if real < width:
                out[at, :, offset + real : offset + width] = jnp.zeros((rows, width - real), BF16)
        out[at, :, 2 * width :] = tail


def up_projected(hidden_in, parts, gain, gate, up, width):
    rows, depth = hidden_in.shape
    return pl.pallas_call(
        functools.partial(up_kernel, width),
        in_specs=whole(RING + 4),
        out_specs=whole(2),
        out_shape=(
            kept((RING, rows, 2 * width + LANES), BF16),
            kept((rows, depth), F32),
        ),
        compiler_params=params(4),
        name="gate_up",
    )(*vmem(hidden_in, *parts, gain, gate, up))


def summed(parts, width):
    total = sum(part[:, : 2 * width].astype(F32) for part in parts)
    tail = sum(part[:, 2 * width :].astype(F32) for part in parts)
    squares = tail[:, :1] + tail[:, LANES // 2 : LANES // 2 + 1]
    return total, squares


def sum_kernel(width, *refs):
    total, squares = summed(refs[:RING], width)
    out = refs[RING]
    out[:, : 2 * width] = total.astype(BF16)
    high = squares.astype(BF16).astype(F32)
    lane = lax.broadcasted_iota(jnp.int32, (total.shape[0], LANES), 1)
    out[:, 2 * width :] = jnp.where(lane < LANES // 2, high, squares - high).astype(BF16)


def summed_terms(parts, width):
    return pl.pallas_call(
        functools.partial(sum_kernel, width),
        in_specs=whole(RING),
        out_specs=whole(1)[0],
        out_shape=kept(parts[0].shape, BF16),
        compiler_params=params(4),
        name="sum_x",
    )(*vmem(*parts))


def hidden_kernel(width, full_width, *refs):
    total, squares = summed(refs[:RING], width)
    out = refs[RING]
    scale = 1.0 / jnp.sqrt(squares / full_width + 1e-05)
    gate_total = total[:, :width] * scale
    up_total = total[:, width:] * scale
    out[...] = (gate_total / (1.0 + jnp.exp(-gate_total)) * up_total).astype(BF16)


def hidden_units(parts, width, full_width):
    return pl.pallas_call(
        functools.partial(hidden_kernel, width, full_width),
        in_specs=whole(RING),
        out_specs=whole(1)[0],
        out_shape=kept((parts[0].shape[0], width), BF16),
        compiler_params=params(4),
        name="sum_z_hidden",
    )(*vmem(*parts))


def down_kernel(*refs):
    parts, weight, own, other, hidden, terms = refs[:RING], *refs[RING:]
    place = ring_index("kvseq", 1)
    core = lax.rem(lax.axis_index("kvhead"), 2)
    for shift in range(RING):
        hidden[lax.rem(place + RING - shift, RING)] = parts[shift][...]
    width = hidden.shape[2]
    depth = weight.shape[0]
    total = None
    for part in range(RING):
        start = part * width
        real = min(width, depth - start)
        term = jnp.dot(
            hidden[part, :, :real], weight[start : start + real, :], preferred_element_type=F32
        )
        total = term if total is None else total + term
    terms[...] = total
    half = own.shape[0]
    own[...] = terms[pl.ds(pl.multiple_of(core * half, half), half), :]
    other[...] = terms[pl.ds(pl.multiple_of((1 - core) * half, half), half), :]


def down_projected(parts, weight):
    rows, width = parts[0].shape
    columns = weight.shape[1]
    half = kept((rows // 2, columns), F32)
    return pl.pallas_call(
        down_kernel,
        in_specs=whole(RING + 1),
        out_specs=whole(2),
        out_shape=(half, half),
        scratch_shapes=[
            pltpu.VMEM((RING, rows, width), BF16),
            pltpu.VMEM((rows, columns), F32),
        ],
        compiler_params=params(4),
        name="down",
    )(*vmem(*parts, weight))


def rows_kernel(own, other, residual, out):
    place = ring_index("kvhead", 2)
    core = lax.rem(lax.axis_index("kvhead"), 2)
    half = own.shape[0]
    mine = residual[pl.ds(pl.multiple_of(core * half, half), half), :]
    total = own[...] + other[...]
    each = half // RING
    for part in range(RING):
        rows = slice(part * each, (part + 1) * each)
        at = lax.rem(part + RING - place, RING)
        out[at] = total[rows] + jnp.where(part == place, mine[rows], 0.0)


def row_chunks(own, other, residual):
    half, columns = own.shape
    return pl.pallas_call(
        rows_kernel,
        in_specs=whole(3),
        out_specs=whole(1)[0],
        out_shape=kept((RING, half // RING, columns), F32),
        compiler_params=params(4),
        name="row_chunks",
    )(*vmem(own, other, residual))


def swapped(part):
    size = lax.axis_size("kvhead")
    return lax.ppermute(part, "kvhead", [(at, at ^ 1) for at in range(size)])


def local(
    hidden_in,
    queries,
    new_keys,
    new_values,
    cache_keys,
    cache_values,
    lengths,
    out_weight,
    norm_gain,
    gate_weight,
    up_weight,
    down_weight,
):
    requests, steps = queries.shape[:2]
    rows = requests * steps
    depth = hidden_in.shape[1]
    full_width = depth * lax.axis_size("kvseq")
    units = gate_weight.shape[1]
    width = -(-units // (RING * LANES)) * LANES
    ordered = (
        hidden_in.reshape(requests, 2, steps // 2, depth).transpose(1, 0, 2, 3).reshape(rows, depth)
    )
    part = attention(queries, new_keys, new_values, cache_keys, cache_values, lengths)
    part = merged([part, *from_others(part, "kvseq", 1)])
    terms = projected([part, *from_others(part, "kvseq", RING)], out_weight, rows)
    pair = (terms + swapped(terms)).astype(BF16)
    chunks, residual = up_projected(
        ordered,
        [pair, *from_others(pair, "kvhead", 2)],
        norm_gain.reshape(1, depth),
        gate_weight,
        up_weight,
        width,
    )
    total = summed_terms([chunks[0], *chunks_from_others(chunks, "kvseq", 1)], width)
    hidden = hidden_units([total, *from_others(total, "kvseq", RING)], width, full_width)
    own, other = down_projected([hidden, *from_others(hidden, "kvseq", 1)], down_weight)
    shares = row_chunks(own, swapped(other), residual)
    received = chunks_from_others(shares, "kvhead", 2)
    return (shares[0] + received[0] + received[1] + received[2]).astype(BF16)


def solution(mesh):
    in_specs = (
        P(None, "kvseq"),
        P(None, None, "kvhead", None),
        P(None, None, "kvhead", None),
        P(None, None, "kvhead", None),
        P(None, "kvseq", "kvhead", None),
        P(None, "kvseq", "kvhead", None),
        P(),
        P("kvhead", "kvseq"),
        P("kvseq"),
        P("kvseq", "kvhead"),
        P("kvseq", "kvhead"),
        P("kvhead", "kvseq"),
    )
    out_specs = P("kvhead", "kvseq")
    return jax.shard_map(local, mesh=mesh, in_specs=in_specs, out_specs=out_specs, check_vma=False)
```

```python
import functools
import math

import jax
import jax.numpy as jnp
from jax import lax
from jax.experimental import pallas as pl
from jax.experimental.pallas import tpu as pltpu
from jax.sharding import PartitionSpec as P

MASKED = -1e30
F32 = jnp.float32
BF16 = jnp.bfloat16
LANES = 128
RING = 4
TURNS = (2, 3, 1)


def ring_index(axis, stride):
    return lax.rem(lax.div(lax.axis_index(axis), stride), RING)


def partner(place, turn):
    return lax.bitwise_xor(place, turn)


def moved(part, axis, stride, turn):
    pairs = []
    for at in range(lax.axis_size(axis)):
        place = (at // stride) % RING
        pairs.append((at, at + ((place ^ turn) - place) * stride))
    return lax.ppermute(part, axis, pairs)


def exchanged(parts, axis, stride):
    received = {turn: moved(parts[turn], axis, stride, turn) for turn in TURNS}
    return [received.get(turn, parts[turn]) for turn in range(RING)]


def vmem(*arrays):
    return [pltpu.with_memory_space_constraint(array, pltpu.VMEM) for array in arrays]


def whole(count):
    return [pl.BlockSpec(memory_space=pltpu.VMEM)] * count


def kept(shape, dtype):
    return pltpu.VMEM(shape, dtype)


def params(mib):
    return pltpu.CompilerParams(vmem_limit_bytes=mib << 20)


def diagonal(size):
    rows = lax.broadcasted_iota(jnp.int32, (size, size), 0)
    columns = lax.broadcasted_iota(jnp.int32, (size, size), 1)
    return rows == columns


def three_parts(value):
    first = value.astype(BF16)
    rest = value - first.astype(F32)
    second = rest.astype(BF16)
    third = (rest - second.astype(F32)).astype(BF16)
    return first.astype(F32), second.astype(F32), third.astype(F32)


def packed_levels(level, rows):
    size = level.shape[0]
    line = jnp.sum(
        jnp.where(diagonal(size), jnp.broadcast_to(level, (size, size)), 0.0), axis=0, keepdims=True
    )
    row = lax.broadcasted_iota(jnp.int32, (rows, size), 0)
    tile = jnp.zeros((rows, size), F32)
    for at, part in enumerate(three_parts(line)):
        tile = jnp.where(row == at, jnp.broadcast_to(part, (rows, size)), tile)
    return tile.astype(BF16)


def attention_kernel(
    lengths,
    query_in,
    keys_in,
    values_in,
    fresh_keys_in,
    fresh_values_in,
    *refs,
):
    extra = (len(refs) - 7) // 2
    extras_in, out, extras = refs[:extra], refs[extra], refs[extra + 1 : 2 * extra + 1]
    query, keys, values, fresh_keys, fresh_values, sems = refs[2 * extra + 1 :]
    requests, rows, head_dim = query.shape
    slots = keys.shape[1]
    steps = fresh_keys.shape[1]
    moves = []
    for source, target in (
        (query_in, query),
        (fresh_keys_in, fresh_keys),
        (keys_in, keys),
        (fresh_values_in, fresh_values),
        (values_in, values),
        *zip(extras_in, extras),
    ):
        moves.append(pltpu.make_async_copy(source, target, sems.at[len(moves)]))
        moves[-1].start()
    shard = lax.axis_index("kvseq")
    count = requests * rows
    fresh = requests * steps
    scale = 1.0 / math.sqrt(head_dim)
    contract = (((1,), (1,)), ((), ()))
    for move in moves[:3]:
        move.wait()
    fresh_row = lax.broadcasted_iota(jnp.int32, (count, fresh), 0)
    token = lax.broadcasted_iota(jnp.int32, (count, fresh), 1)
    per_step = rows // steps
    row_step = lax.div(fresh_row, per_step)
    same_request = lax.div(row_step, steps) == lax.div(token, steps)
    fresh_mask = same_request & (token <= jnp.where(shard == 0, row_step, -1))
    flat_keys = jnp.concatenate(
        [fresh_keys[request].astype(F32) for request in range(requests)], axis=0
    ).astype(BF16)
    everyone = jnp.concatenate([query[request] for request in range(requests)], axis=0)
    fresh_scores = jnp.where(
        fresh_mask,
        lax.dot_general(everyone, flat_keys, contract, preferred_element_type=F32) * scale,
        MASKED,
    )
    fresh_top = jnp.max(fresh_scores, axis=1, keepdims=True)
    slot = lax.broadcasted_iota(jnp.int32, (rows, slots), 1)
    tops, probs, totals = [], [], []
    for request in range(requests):
        mine = slice(request * rows, (request + 1) * rows)
        mask = slot < lengths[request] - shard * slots
        scores = jnp.where(
            mask,
            lax.dot_general(query[request], keys[request], contract, preferred_element_type=F32)
            * scale,
            MASKED,
        )
        top = jnp.maximum(jnp.max(scores, axis=1, keepdims=True), fresh_top[mine])
        prob = jnp.where(mask, jnp.exp(scores - top), 0.0)
        tops.append(top)
        totals.append(jnp.sum(prob, axis=1, keepdims=True))
        probs.append(prob.astype(BF16))
    top = jnp.concatenate(tops, axis=0)
    fresh_prob = jnp.where(fresh_mask, jnp.exp(fresh_scores - top), 0.0)
    total = jnp.concatenate(totals, axis=0) + jnp.sum(fresh_prob, axis=1, keepdims=True)
    for move in moves[3:5]:
        move.wait()
    flat_values = jnp.concatenate(
        [fresh_values[request].astype(F32) for request in range(requests)], axis=0
    ).astype(BF16)
    weighted = jnp.dot(fresh_prob.astype(BF16), flat_values, preferred_element_type=F32)
    weighted = weighted + jnp.concatenate(
        [
            jnp.dot(probs[request], values[request], preferred_element_type=F32)
            for request in range(requests)
        ],
        axis=0,
    )
    some = total > 0.0
    safe = jnp.where(some, total, 1.0)
    mean = weighted / safe
    level = jnp.where(some, top + jnp.log(safe), MASKED)
    half = rows // 2
    order = [
        slice(request * rows + part * half, request * rows + (part + 1) * half)
        for part in range(2)
        for request in range(requests)
    ]
    mean = jnp.concatenate([mean[rows_of] for rows_of in order], axis=0)
    level = jnp.concatenate([level[rows_of] for rows_of in order], axis=0)
    out[:count, :] = mean.astype(BF16)
    out[count:, :] = packed_levels(level, 16)
    for move in moves[5:]:
        move.wait()


def hbm(*arrays):
    return [pltpu.with_memory_space_constraint(array, pltpu.HBM) for array in arrays]


def anywhere(count):
    return [pl.BlockSpec(memory_space=pl.ANY)] * count


def attention(queries, new_keys, new_values, cache_keys, cache_values, lengths, extras):
    requests, slots, _, head_dim = cache_keys.shape
    rows = queries.shape[1] * queries.shape[2]
    steps = new_keys.shape[1]
    shapes = [
        (requests, rows, head_dim),
        (requests, slots, head_dim),
        (requests, slots, head_dim),
        (requests, steps, head_dim),
        (requests, steps, head_dim),
    ]
    arrays = (queries, cache_keys, cache_values, new_keys, new_values)
    return pl.pallas_call(
        attention_kernel,
        in_specs=[pl.BlockSpec(memory_space=pltpu.SMEM), *anywhere(5 + len(extras))],
        out_specs=whole(1 + len(extras)),
        out_shape=(
            kept((requests * rows + 16, head_dim), BF16),
            *(kept(extra.shape, extra.dtype) for extra in extras),
        ),
        scratch_shapes=[
            *(pltpu.VMEM(shape, BF16) for shape in shapes),
            pltpu.SemaphoreType.DMA((5 + len(extras),)),
        ],
        compiler_params=params(8),
        name="attention",
    )(
        *hbm(lengths, *(array.reshape(shape) for array, shape in zip(arrays, shapes)), *extras),
    )


def fetch_kernel(count, *refs):
    sources, targets, sems = refs[:count], refs[count + 1 : 2 * count + 1], refs[2 * count + 1]
    moves = []
    for source, target in zip(sources, targets):
        rows = source.shape[0]
        pieces = 4 if rows % 64 == 0 else 1
        for piece in range(pieces):
            part = pl.ds(piece * (rows // pieces), rows // pieces)
            moves.append(
                pltpu.make_async_copy(source.at[part], target.at[part], sems.at[len(moves)])
            )
            moves[-1].start()
    for move in moves:
        move.wait()


def fetched(arrays, after):
    count = len(arrays)
    moved_bytes = sum(array.size * array.dtype.itemsize for array in arrays)
    return pl.pallas_call(
        functools.partial(fetch_kernel, count),
        in_specs=anywhere(count + 1),
        out_specs=whole(count),
        out_shape=tuple(kept(array.shape, array.dtype) for array in arrays),
        scratch_shapes=[pltpu.SemaphoreType.DMA((4 * count,))],
        compiler_params=params(1),
        cost_estimate=pl.CostEstimate(flops=0, transcendentals=0, bytes_accessed=2 * moved_bytes),
        name="fetch",
    )(*hbm(*arrays), after)


def merge(parts):
    count = parts[0].shape[0] - 16
    same = diagonal(count)
    levels, means = [], []
    for part in parts:
        tail = part[count:, :].astype(F32)
        line = tail[0:1] + tail[1:2] + tail[2:3]
        levels.append(
            jnp.sum(
                jnp.where(same, jnp.broadcast_to(line, (count, count)), 0.0), axis=1, keepdims=True
            )
        )
        means.append(part[:count, :].astype(F32))
    top = functools.reduce(jnp.maximum, levels)
    scales = [jnp.exp(level - top) for level in levels]
    total = sum(scales)
    mean = sum(scale * mean for scale, mean in zip(scales, means)) / total
    return mean, top + jnp.log(total)


def merge_kernel(*refs):
    parts, out = refs[:RING], refs[RING + 1]
    mean, level = merge(parts)
    count = mean.shape[0]
    out[:count, :] = mean.astype(BF16)
    out[count:, :] = packed_levels(level, 16)


def merged(parts, after):
    return pl.pallas_call(
        merge_kernel,
        in_specs=whole(RING + 1),
        out_specs=whole(1)[0],
        out_shape=kept(parts[0].shape, BF16),
        compiler_params=params(4),
        name="merge_x",
    )(*vmem(*parts, after))


def project_kernel(*refs):
    parts, weight, out, attended = refs[:RING], refs[RING], refs[RING + 1], refs[RING + 2]
    mean, _ = merge(parts)
    attended[...] = mean
    rows = out.shape[0]
    heads = mean.shape[0] // rows
    row = jnp.concatenate(
        [attended[pl.ds(head, rows, stride=heads), :].astype(BF16) for head in range(heads)], axis=1
    )
    out[...] = jnp.dot(row, weight[...], preferred_element_type=F32)


def projected(parts, weight, rows):
    count, head_dim = parts[0].shape
    return pl.pallas_call(
        project_kernel,
        in_specs=whole(RING + 1),
        out_specs=whole(1)[0],
        out_shape=kept((rows, weight.shape[1]), F32),
        scratch_shapes=[pltpu.VMEM((count - 16, head_dim), F32)],
        compiler_params=params(4),
        name="merge_z_project",
    )(*vmem(*parts, weight))


def up_kernel(width, hidden_in, first, second, third, fourth, gain, gate, up, out, residual):
    place = ring_index("kvseq", 1)
    before = hidden_in[...].astype(F32)
    pair = before.shape[0] // (2 * RING)
    before = jnp.concatenate(
        [
            before[(2 * request + part) * pair : (2 * request + part + 1) * pair]
            for part in range(2)
            for request in range(RING)
        ],
        axis=0,
    )
    total = (
        before
        + first[...].astype(F32)
        + second[...].astype(F32)
        + third[...].astype(F32)
        + fourth[...].astype(F32)
    )
    residual[...] = total
    squares = jnp.sum(total * total, axis=1, keepdims=True)
    high = squares.astype(BF16).astype(F32)
    rows = total.shape[0]
    lane = lax.broadcasted_iota(jnp.int32, (rows, LANES), 1)
    tail = jnp.where(lane < LANES // 2, high, squares - high).astype(BF16)
    scaled = (total * gain[...]).astype(BF16)
    columns = gate.shape[1]
    for part in range(RING):
        start = part * width
        real = min(width, columns - start)
        at = partner(place, part)
        for offset, weight in ((0, gate), (width, up)):
            terms = jnp.dot(scaled, weight[:, start : start + real], preferred_element_type=F32)
            out[at, :, offset : offset + real] = terms.astype(BF16)
            if real < width:
                out[at, :, offset + real : offset + width] = jnp.zeros((rows, width - real), BF16)
        out[at, :, 2 * width :] = tail


def up_projected(hidden_in, parts, gain, gate, up, width):
    rows, depth = hidden_in.shape
    return pl.pallas_call(
        functools.partial(up_kernel, width),
        in_specs=whole(RING + 4),
        out_specs=whole(2),
        out_shape=(
            kept((RING, rows, 2 * width + LANES), BF16),
            kept((rows, depth), F32),
        ),
        compiler_params=params(4),
        name="gate_up",
    )(*vmem(hidden_in, *parts, gain, gate, up))


def summed(parts, width):
    total = sum(part[:, : 2 * width].astype(F32) for part in parts)
    tail = sum(part[:, 2 * width :].astype(F32) for part in parts)
    squares = tail[:, :1] + tail[:, LANES // 2 : LANES // 2 + 1]
    return total, squares


def sum_kernel(width, *refs):
    total, squares = summed(refs[:RING], width)
    out = refs[RING]
    out[:, : 2 * width] = total.astype(BF16)
    high = squares.astype(BF16).astype(F32)
    lane = lax.broadcasted_iota(jnp.int32, (total.shape[0], LANES), 1)
    out[:, 2 * width :] = jnp.where(lane < LANES // 2, high, squares - high).astype(BF16)


def summed_terms(parts, width):
    return pl.pallas_call(
        functools.partial(sum_kernel, width),
        in_specs=whole(RING),
        out_specs=whole(1)[0],
        out_shape=kept(parts[0].shape, BF16),
        compiler_params=params(4),
        name="sum_x",
    )(*vmem(*parts))


def hidden_kernel(width, full_width, *refs):
    total, squares = summed(refs[:RING], width)
    out = refs[RING]
    scale = 1.0 / jnp.sqrt(squares / full_width + 1e-05)
    gate_total = total[:, :width] * scale
    up_total = total[:, width:] * scale
    out[...] = (gate_total / (1.0 + jnp.exp(-gate_total)) * up_total).astype(BF16)


def hidden_units(parts, width, full_width):
    return pl.pallas_call(
        functools.partial(hidden_kernel, width, full_width),
        in_specs=whole(RING),
        out_specs=whole(1)[0],
        out_shape=kept((parts[0].shape[0], width), BF16),
        compiler_params=params(4),
        name="sum_z_hidden",
    )(*vmem(*parts))


def down_kernel(*refs):
    parts, weight, own, other, hidden, terms = refs[:RING], *refs[RING:]
    place = ring_index("kvseq", 1)
    core = lax.rem(lax.axis_index("kvhead"), 2)
    for turn in range(RING):
        hidden[partner(place, turn)] = parts[turn][...]
    width = hidden.shape[2]
    depth = weight.shape[0]
    total = None
    for part in range(RING):
        start = part * width
        real = min(width, depth - start)
        term = jnp.dot(
            hidden[part, :, :real], weight[start : start + real, :], preferred_element_type=F32
        )
        total = term if total is None else total + term
    terms[...] = total
    half = own.shape[0]
    own[...] = terms[pl.ds(pl.multiple_of(core * half, half), half), :]
    other[...] = terms[pl.ds(pl.multiple_of((1 - core) * half, half), half), :]


def down_projected(parts, weight):
    rows, width = parts[0].shape
    columns = weight.shape[1]
    half = kept((rows // 2, columns), F32)
    return pl.pallas_call(
        down_kernel,
        in_specs=whole(RING + 1),
        out_specs=whole(2),
        out_shape=(half, half),
        scratch_shapes=[
            pltpu.VMEM((RING, rows, width), BF16),
            pltpu.VMEM((rows, columns), F32),
        ],
        compiler_params=params(4),
        name="down",
    )(*vmem(*parts, weight))


def rows_kernel(own, other, residual, out):
    place = ring_index("kvhead", 2)
    core = lax.rem(lax.axis_index("kvhead"), 2)
    half = own.shape[0]
    mine = residual[pl.ds(pl.multiple_of(core * half, half), half), :]
    total = own[...] + other[...]
    each = half // RING
    for part in range(RING):
        rows = slice(part * each, (part + 1) * each)
        at = partner(place, part)
        out[at] = total[rows] + jnp.where(part == place, mine[rows], 0.0)


def row_chunks(own, other, residual):
    half, columns = own.shape
    return pl.pallas_call(
        rows_kernel,
        in_specs=whole(3),
        out_specs=whole(1)[0],
        out_shape=kept((RING, half // RING, columns), F32),
        compiler_params=params(4),
        name="row_chunks",
    )(*vmem(own, other, residual))


def swapped(part):
    size = lax.axis_size("kvhead")
    return lax.ppermute(part, "kvhead", [(at, at ^ 1) for at in range(size)])


def local(
    hidden_in,
    queries,
    new_keys,
    new_values,
    cache_keys,
    cache_values,
    lengths,
    out_weight,
    norm_gain,
    gate_weight,
    up_weight,
    down_weight,
):
    requests, steps = queries.shape[:2]
    rows = requests * steps
    depth = hidden_in.shape[1]
    full_width = depth * lax.axis_size("kvseq")
    units = gate_weight.shape[1]
    width = -(-units // (RING * LANES)) * LANES
    part, out_held, hidden_held = attention(
        queries,
        new_keys,
        new_values,
        cache_keys,
        cache_values,
        lengths,
        [out_weight, hidden_in],
    )
    gate_held, gain_held = fetched([gate_weight, norm_gain.reshape(1, depth)], part)
    part = merged(exchanged([part] * RING, "kvseq", 1), gain_held)
    (up_held,) = fetched([up_weight], part)
    terms = projected(exchanged([part] * RING, "kvseq", RING), out_held, rows)
    pair = (terms + swapped(terms)).astype(BF16)
    (down_held,) = fetched([down_weight], pair)
    chunks, residual = up_projected(
        hidden_held, exchanged([pair] * RING, "kvhead", 2), gain_held, gate_held, up_held, width
    )
    total = summed_terms(exchanged(chunks, "kvseq", 1), width)
    hidden = hidden_units(exchanged([total] * RING, "kvseq", RING), width, full_width)
    own, other = down_projected(exchanged([hidden] * RING, "kvseq", 1), down_held)
    shares = exchanged(row_chunks(own, swapped(other), residual), "kvhead", 2)
    return sum(shares).astype(BF16)


def solution(mesh):
    in_specs = (
        P(None, "kvseq"),
        P(None, None, "kvhead", None),
        P(None, None, "kvhead", None),
        P(None, None, "kvhead", None),
        P(None, "kvseq", "kvhead", None),
        P(None, "kvseq", "kvhead", None),
        P(),
        P("kvhead", "kvseq"),
        P("kvseq"),
        P("kvseq", "kvhead"),
        P("kvseq", "kvhead"),
        P("kvhead", "kvseq"),
    )
    out_specs = P("kvhead", "kvseq")
    return jax.shard_map(local, mesh=mesh, in_specs=in_specs, out_specs=out_specs, check_vma=False)
```

```python
import functools
import math

import jax
import jax.numpy as jnp
from jax import lax
from jax.experimental import pallas as pl
from jax.experimental.pallas import tpu as pltpu
from jax.sharding import PartitionSpec as P

MASKED = -1e30
F32 = jnp.float32
BF16 = jnp.bfloat16
LANES = 128
RING = 4
USE = (0, 3, 2, 1)
ORDER = (3, 2, 1)


def ring_index(axis, stride):
    return lax.rem(lax.div(lax.axis_index(axis), stride), RING)


def partner(place, turn):
    return lax.bitwise_xor(place, turn)


def moved(part, axis, stride, turn):
    pairs = []
    for at in range(lax.axis_size(axis)):
        place = (at // stride) % RING
        pairs.append((at, at + ((place ^ turn) - place) * stride))
    return lax.ppermute(part, axis, pairs)


def exchanged(parts, axis, stride):
    received = {turn: moved(parts[turn], axis, stride, turn) for turn in ORDER}
    return [received.get(turn, parts[turn]) for turn in range(RING)]


def vmem(*arrays):
    return [pltpu.with_memory_space_constraint(array, pltpu.VMEM) for array in arrays]


def whole(count):
    return [pl.BlockSpec(memory_space=pltpu.VMEM)] * count


def kept(shape, dtype):
    return pltpu.VMEM(shape, dtype)


def params(mib):
    return pltpu.CompilerParams(vmem_limit_bytes=mib << 20)


def diagonal(size):
    rows = lax.broadcasted_iota(jnp.int32, (size, size), 0)
    columns = lax.broadcasted_iota(jnp.int32, (size, size), 1)
    return rows == columns


def three_parts(value):
    first = value.astype(BF16)
    rest = value - first.astype(F32)
    second = rest.astype(BF16)
    third = (rest - second.astype(F32)).astype(BF16)
    return first.astype(F32), second.astype(F32), third.astype(F32)


def packed_levels(level, rows):
    size = level.shape[0]
    line = jnp.sum(
        jnp.where(diagonal(size), jnp.broadcast_to(level, (size, size)), 0.0), axis=0, keepdims=True
    )
    row = lax.broadcasted_iota(jnp.int32, (rows, size), 0)
    tile = jnp.zeros((rows, size), F32)
    for at, part in enumerate(three_parts(line)):
        tile = jnp.where(row == at, jnp.broadcast_to(part, (rows, size)), tile)
    return tile.astype(BF16)


def attention_kernel(
    lengths_in,
    query_in,
    keys_in,
    values_in,
    fresh_keys_in,
    fresh_values_in,
    *refs,
):
    extra = (len(refs) - 8) // 2
    extras_in, out, extras = refs[:extra], refs[extra], refs[extra + 1 : 2 * extra + 1]
    lengths, query, keys, values, fresh_keys, fresh_values, sems = refs[2 * extra + 1 :]
    requests, rows, head_dim = query.shape
    slots = keys.shape[1]
    steps = fresh_keys.shape[1]
    moves = []
    for source, target in (
        (lengths_in, lengths),
        (query_in, query),
        (fresh_keys_in, fresh_keys),
        (keys_in, keys),
        (fresh_values_in, fresh_values),
        (values_in, values),
        *zip(extras_in, extras),
    ):
        moves.append(pltpu.make_async_copy(source, target, sems.at[len(moves)]))
        moves[-1].start()
    shard = lax.axis_index("kvseq")
    count = requests * rows
    fresh = requests * steps
    scale = 1.0 / math.sqrt(head_dim)
    contract = (((1,), (1,)), ((), ()))
    for move in moves[:4]:
        move.wait()
    fresh_row = lax.broadcasted_iota(jnp.int32, (count, fresh), 0)
    token = lax.broadcasted_iota(jnp.int32, (count, fresh), 1)
    per_step = rows // steps
    row_step = lax.div(fresh_row, per_step)
    same_request = lax.div(row_step, steps) == lax.div(token, steps)
    fresh_mask = same_request & (token <= jnp.where(shard == 0, row_step, -1))
    flat_keys = jnp.concatenate(
        [fresh_keys[request].astype(F32) for request in range(requests)], axis=0
    ).astype(BF16)
    everyone = jnp.concatenate([query[request] for request in range(requests)], axis=0)
    fresh_scores = jnp.where(
        fresh_mask,
        lax.dot_general(everyone, flat_keys, contract, preferred_element_type=F32) * scale,
        MASKED,
    )
    fresh_top = jnp.max(fresh_scores, axis=1, keepdims=True)
    slot = lax.broadcasted_iota(jnp.int32, (rows, slots), 1)
    tops, probs, totals = [], [], []
    for request in range(requests):
        mine = slice(request * rows, (request + 1) * rows)
        mask = slot < lengths[request] - shard * slots
        scores = jnp.where(
            mask,
            lax.dot_general(query[request], keys[request], contract, preferred_element_type=F32)
            * scale,
            MASKED,
        )
        top = jnp.maximum(jnp.max(scores, axis=1, keepdims=True), fresh_top[mine])
        prob = jnp.where(mask, jnp.exp(scores - top), 0.0)
        tops.append(top)
        totals.append(jnp.sum(prob, axis=1, keepdims=True))
        probs.append(prob.astype(BF16))
    top = jnp.concatenate(tops, axis=0)
    fresh_prob = jnp.where(fresh_mask, jnp.exp(fresh_scores - top), 0.0)
    total = jnp.concatenate(totals, axis=0) + jnp.sum(fresh_prob, axis=1, keepdims=True)
    for move in moves[4:6]:
        move.wait()
    flat_values = jnp.concatenate(
        [fresh_values[request].astype(F32) for request in range(requests)], axis=0
    ).astype(BF16)
    weighted = jnp.dot(fresh_prob.astype(BF16), flat_values, preferred_element_type=F32)
    weighted = weighted + jnp.concatenate(
        [
            jnp.dot(probs[request], values[request], preferred_element_type=F32)
            for request in range(requests)
        ],
        axis=0,
    )
    some = total > 0.0
    safe = jnp.where(some, total, 1.0)
    mean = weighted / safe
    level = jnp.where(some, top + jnp.log(safe), MASKED)
    half = rows // 2
    order = [
        slice(request * rows + part * half, request * rows + (part + 1) * half)
        for part in range(2)
        for request in range(requests)
    ]
    mean = jnp.concatenate([mean[rows_of] for rows_of in order], axis=0)
    level = jnp.concatenate([level[rows_of] for rows_of in order], axis=0)
    out[:count, :] = mean.astype(BF16)
    out[count:, :] = packed_levels(level, 16)
    for move in moves[6:]:
        move.wait()


def hbm(*arrays):
    return [pltpu.with_memory_space_constraint(array, pltpu.HBM) for array in arrays]


def anywhere(count):
    return [pl.BlockSpec(memory_space=pl.ANY)] * count


def attention(queries, new_keys, new_values, cache_keys, cache_values, lengths, extras):
    requests, slots, _, head_dim = cache_keys.shape
    rows = queries.shape[1] * queries.shape[2]
    steps = new_keys.shape[1]
    shapes = [
        (requests, rows, head_dim),
        (requests, slots, head_dim),
        (requests, slots, head_dim),
        (requests, steps, head_dim),
        (requests, steps, head_dim),
    ]
    arrays = (queries, cache_keys, cache_values, new_keys, new_values)
    return pl.pallas_call(
        attention_kernel,
        in_specs=anywhere(6 + len(extras)),
        out_specs=whole(1 + len(extras)),
        out_shape=(
            kept((requests * rows + 16, head_dim), BF16),
            *(kept(extra.shape, extra.dtype) for extra in extras),
        ),
        scratch_shapes=[
            pltpu.SMEM(lengths.shape, lengths.dtype),
            *(pltpu.VMEM(shape, BF16) for shape in shapes),
            pltpu.SemaphoreType.DMA((6 + len(extras),)),
        ],
        compiler_params=params(8),
        name="attention",
    )(
        *hbm(lengths, *(array.reshape(shape) for array, shape in zip(arrays, shapes)), *extras),
    )


def fetch_kernel(count, *refs):
    sources, targets, sems = refs[:count], refs[count + 1 : 2 * count + 1], refs[2 * count + 1]
    moves = []
    for source, target in zip(sources, targets):
        rows = source.shape[0]
        pieces = 4 if rows % 64 == 0 else 1
        for piece in range(pieces):
            part = pl.ds(piece * (rows // pieces), rows // pieces)
            moves.append(
                pltpu.make_async_copy(source.at[part], target.at[part], sems.at[len(moves)])
            )
            moves[-1].start()
    for move in moves:
        move.wait()


def fetched(arrays, after):
    count = len(arrays)
    moved_bytes = sum(array.size * array.dtype.itemsize for array in arrays)
    return pl.pallas_call(
        functools.partial(fetch_kernel, count),
        in_specs=anywhere(count + 1),
        out_specs=whole(count),
        out_shape=tuple(kept(array.shape, array.dtype) for array in arrays),
        scratch_shapes=[pltpu.SemaphoreType.DMA((4 * count,))],
        compiler_params=params(1),
        cost_estimate=pl.CostEstimate(flops=0, transcendentals=0, bytes_accessed=2 * moved_bytes),
        name="fetch",
    )(*hbm(*arrays), after)


def merge(parts):
    count = parts[0].shape[0] - 16
    same = diagonal(count)
    levels, means = [], []
    for part in parts:
        tail = part[count:, :].astype(F32)
        line = tail[0:1] + tail[1:2] + tail[2:3]
        levels.append(
            jnp.sum(
                jnp.where(same, jnp.broadcast_to(line, (count, count)), 0.0), axis=1, keepdims=True
            )
        )
        means.append(part[:count, :].astype(F32))
    top = functools.reduce(jnp.maximum, levels)
    scales = [jnp.exp(level - top) for level in levels]
    total = sum(scales)
    mean = sum(scale * mean for scale, mean in zip(scales, means)) / total
    return mean, top + jnp.log(total)


def merge_kernel(*refs):
    parts, out = refs[:RING], refs[RING + 1]
    mean, level = merge(parts)
    count = mean.shape[0]
    out[:count, :] = mean.astype(BF16)
    out[count:, :] = packed_levels(level, 16)


def merged(parts, after):
    return pl.pallas_call(
        merge_kernel,
        in_specs=whole(RING + 1),
        out_specs=whole(1)[0],
        out_shape=kept(parts[0].shape, BF16),
        compiler_params=params(4),
        name="merge_x",
    )(*vmem(*parts, after))


def project_kernel(*refs):
    parts, (weight, _, out, attended) = refs[:RING], refs[RING:]
    mean, _ = merge(parts)
    attended[...] = mean
    rows = out.shape[0]
    heads = mean.shape[0] // rows
    row = jnp.concatenate(
        [attended[pl.ds(head, rows, stride=heads), :].astype(BF16) for head in range(heads)], axis=1
    )
    out[...] = jnp.dot(row, weight[...], preferred_element_type=F32)


def projected(parts, weight, rows, after):
    count, head_dim = parts[0].shape
    return pl.pallas_call(
        project_kernel,
        in_specs=[*whole(RING + 1), *anywhere(1)],
        out_specs=whole(1)[0],
        out_shape=kept((rows, weight.shape[1]), F32),
        scratch_shapes=[pltpu.VMEM((count - 16, head_dim), F32)],
        compiler_params=params(4),
        name="merge_z_project",
    )(*vmem(*parts, weight, after))


def quarter_start(quarter, width, size):
    return pl.multiple_of(jnp.minimum(quarter * width, size - width), LANES)


def chunk_into(out, scaled, tail, gate, up, turn):
    width = (out.shape[1] - LANES) // 2
    quarter = partner(ring_index("kvseq", 1), turn)
    columns = pl.ds(quarter_start(quarter, width, gate.shape[1]), width)
    for offset, weight in ((0, gate), (width, up)):
        out[:, offset : offset + width] = jnp.dot(
            scaled, weight[:, columns], preferred_element_type=F32
        ).astype(BF16)
    out[:, 2 * width :] = tail


def first_up_kernel(hidden_in, *refs):
    parts, (gain, gate, up, _, *refs) = refs[:RING], refs[RING:]
    outs, (residual, scaled, tail) = refs[: RING - 1], refs[RING - 1 :]
    before = hidden_in[...].astype(F32)
    pair = before.shape[0] // (2 * RING)
    before = jnp.concatenate(
        [
            before[(2 * request + part) * pair : (2 * request + part + 1) * pair]
            for part in range(2)
            for request in range(RING)
        ],
        axis=0,
    )
    total = before + sum(part[...].astype(F32) for part in parts)
    residual[...] = total
    squares = jnp.sum(total * total, axis=1, keepdims=True)
    high = squares.astype(BF16).astype(F32)
    lane = lax.broadcasted_iota(jnp.int32, (total.shape[0], LANES), 1)
    tail[...] = jnp.where(lane < LANES // 2, high, squares - high).astype(BF16)
    scaled[...] = (total * gain[...]).astype(BF16)
    for turn, out in enumerate(outs, 1):
        chunk_into(out, scaled[...], tail[...], gate, up, turn)


def own_up_kernel(scaled, tail, gate, up, out):
    chunk_into(out, scaled[...], tail[...], gate, up, 0)


def up_projected(hidden_in, parts, gain, gate, up, width, after):
    rows, depth = hidden_in.shape
    chunk = kept((rows, 2 * width + LANES), BF16)
    *chunks, residual, scaled, tail = pl.pallas_call(
        first_up_kernel,
        in_specs=[*whole(RING + 4), *anywhere(1)],
        out_specs=whole(RING + 2),
        out_shape=(
            *[chunk] * (RING - 1),
            kept((rows, depth), F32),
            kept((rows, depth), BF16),
            kept((rows, LANES), BF16),
        ),
        compiler_params=params(4),
        name="gate_up_others",
    )(*vmem(hidden_in, *parts, gain, gate, up, after))
    own = pl.pallas_call(
        own_up_kernel,
        in_specs=whole(4),
        out_specs=whole(1)[0],
        out_shape=chunk,
        compiler_params=params(4),
        name="gate_up_own",
    )(*vmem(scaled, tail, gate, up))
    return [own, *chunks], residual


def summed(parts, width):
    total = sum(part[:, : 2 * width].astype(F32) for part in parts)
    tail = sum(part[:, 2 * width :].astype(F32) for part in parts)
    squares = tail[:, :1] + tail[:, LANES // 2 : LANES // 2 + 1]
    return total, squares


def sum_kernel(width, *refs):
    total, squares = summed(refs[:RING], width)
    out = refs[RING]
    out[:, : 2 * width] = total.astype(BF16)
    high = squares.astype(BF16).astype(F32)
    lane = lax.broadcasted_iota(jnp.int32, (total.shape[0], LANES), 1)
    out[:, 2 * width :] = jnp.where(lane < LANES // 2, high, squares - high).astype(BF16)


def summed_terms(parts, width):
    return pl.pallas_call(
        functools.partial(sum_kernel, width),
        in_specs=whole(RING),
        out_specs=whole(1)[0],
        out_shape=kept(parts[0].shape, BF16),
        compiler_params=params(4),
        name="sum_x",
    )(*vmem(*parts))


def hidden_kernel(width, full_width, units, *refs):
    total, squares = summed(refs[:RING], width)
    out = refs[RING]
    scale = 1.0 / jnp.sqrt(squares / full_width + 1e-05)
    gate_total = total[:, :width] * scale
    up_total = total[:, width:] * scale
    hidden = gate_total / (1.0 + jnp.exp(-gate_total)) * up_total
    quarter = ring_index("kvseq", 1)
    twice = quarter * width - quarter_start(quarter, width, units)
    lane = lax.broadcasted_iota(jnp.int32, hidden.shape, 1)
    out[...] = jnp.where(lane < twice, 0.0, hidden).astype(BF16)


def hidden_units(parts, width, full_width, units):
    return pl.pallas_call(
        functools.partial(hidden_kernel, width, full_width, units),
        in_specs=whole(RING),
        out_specs=whole(1)[0],
        out_shape=kept((parts[0].shape[0], width), BF16),
        compiler_params=params(4),
        name="sum_z_hidden",
    )(*vmem(*parts))


def down_term(hidden, weight, turn):
    width = hidden.shape[1]
    quarter = partner(ring_index("kvseq", 1), turn)
    rows = pl.ds(quarter_start(quarter, width, weight.shape[0]), width)
    return jnp.dot(hidden[...], weight[rows, :], preferred_element_type=F32)


def first_down_kernel(hidden, weight, out):
    out[...] = down_term(hidden, weight, 0)


def next_down_kernel(turn, before, hidden, weight, out):
    out[...] = before[...] + down_term(hidden, weight, turn)


def last_down_kernel(turn, before, hidden, weight, own, other, terms):
    core = lax.rem(lax.axis_index("kvhead"), 2)
    terms[...] = before[...] + down_term(hidden, weight, turn)
    half = own.shape[0]
    own[...] = terms[pl.ds(pl.multiple_of(core * half, half), half), :]
    other[...] = terms[pl.ds(pl.multiple_of((1 - core) * half, half), half), :]


def down_projected(parts, weight):
    rows, columns = parts[0].shape[0], weight.shape[1]
    full, half = kept((rows, columns), F32), kept((rows // 2, columns), F32)
    terms = pl.pallas_call(
        first_down_kernel,
        in_specs=whole(2),
        out_specs=whole(1)[0],
        out_shape=full,
        compiler_params=params(4),
        name="down_0",
    )(*vmem(parts[0], weight))
    for turn in ORDER[:-1]:
        terms = pl.pallas_call(
            functools.partial(next_down_kernel, turn),
            in_specs=whole(3),
            out_specs=whole(1)[0],
            out_shape=full,
            compiler_params=params(4),
            name=f"down_{turn}",
        )(*vmem(terms, parts[turn], weight))
    return pl.pallas_call(
        functools.partial(last_down_kernel, ORDER[-1]),
        in_specs=whole(3),
        out_specs=whole(2),
        out_shape=(half, half),
        scratch_shapes=[pltpu.VMEM((rows, columns), F32)],
        compiler_params=params(4),
        name="down_last",
    )(*vmem(terms, parts[ORDER[-1]], weight))


def rows_kernel(own, other, residual, *refs):
    outs, held = refs[:RING], refs[RING]
    place = ring_index("kvhead", 2)
    core = lax.rem(lax.axis_index("kvhead"), 2)
    half = own.shape[0]
    mine = residual[pl.ds(pl.multiple_of(core * half, half), half), :]
    total = own[...] + other[...]
    each = half // RING
    for part in range(RING):
        rows = slice(part * each, (part + 1) * each)
        held[part] = total[rows] + jnp.where(part == place, mine[rows], 0.0)
    for turn in range(RING):
        outs[turn][...] = held[partner(place, turn)]


def row_chunks(own, other, residual):
    half, columns = own.shape
    each = half // RING
    return pl.pallas_call(
        rows_kernel,
        in_specs=whole(3),
        out_specs=whole(RING),
        out_shape=(kept((each, columns), F32),) * RING,
        scratch_shapes=[pltpu.VMEM((RING, each, columns), F32)],
        compiler_params=params(4),
        name="row_chunks",
    )(*vmem(own, other, residual))


def row_sum_kernel(first, second, third, fourth, out):
    out[...] = (first[...] + second[...] + third[...] + fourth[...]).astype(BF16)


def row_sum(parts):
    return pl.pallas_call(
        row_sum_kernel,
        in_specs=whole(RING),
        out_specs=whole(1)[0],
        out_shape=jax.ShapeDtypeStruct(parts[0].shape, BF16),
        compiler_params=params(1),
        name="row_sum",
    )(*vmem(*parts))


def swapped(part):
    size = lax.axis_size("kvhead")
    return lax.ppermute(part, "kvhead", [(at, at ^ 1) for at in range(size)])


def local(
    hidden_in,
    queries,
    new_keys,
    new_values,
    cache_keys,
    cache_values,
    lengths,
    out_weight,
    norm_gain,
    gate_weight,
    up_weight,
    down_weight,
):
    requests, steps = queries.shape[:2]
    rows = requests * steps
    depth = hidden_in.shape[1]
    full_width = depth * lax.axis_size("kvseq")
    units = gate_weight.shape[1]
    width = -(-units // (RING * LANES)) * LANES
    part, out_held, hidden_held = attention(
        queries,
        new_keys,
        new_values,
        cache_keys,
        cache_values,
        lengths,
        [out_weight, hidden_in],
    )
    gate_held, gain_held = fetched([gate_weight, norm_gain.reshape(1, depth)], part)
    part = merged(exchanged([part] * RING, "kvseq", 1), gain_held)
    (up_held,) = fetched([up_weight], part)
    terms = projected(exchanged([part] * RING, "kvseq", RING), out_held, rows, up_held)
    pair = (terms + swapped(terms)).astype(BF16)
    (down_held,) = fetched([down_weight], pair)
    chunks, residual = up_projected(
        hidden_held,
        exchanged([pair] * RING, "kvhead", 2),
        gain_held,
        gate_held,
        up_held,
        width,
        down_held,
    )
    received = exchanged(chunks, "kvseq", 1)
    total = summed_terms([received[turn] for turn in USE], width)
    hidden = hidden_units(exchanged([total] * RING, "kvseq", RING), width, full_width, units)
    own, other = down_projected(exchanged([hidden] * RING, "kvseq", 1), down_held)
    shares = exchanged(row_chunks(own, swapped(other), residual), "kvhead", 2)
    return row_sum([shares[turn] for turn in USE])


def solution(mesh):
    in_specs = (
        P(None, "kvseq"),
        P(None, None, "kvhead", None),
        P(None, None, "kvhead", None),
        P(None, None, "kvhead", None),
        P(None, "kvseq", "kvhead", None),
        P(None, "kvseq", "kvhead", None),
        P(),
        P("kvhead", "kvseq"),
        P("kvseq"),
        P("kvseq", "kvhead"),
        P("kvseq", "kvhead"),
        P("kvhead", "kvseq"),
    )
    out_specs = P("kvhead", "kvseq")
    return jax.shard_map(local, mesh=mesh, in_specs=in_specs, out_specs=out_specs, check_vma=False)
```

```python
import functools
import math

import jax
import jax.numpy as jnp
from jax import lax
from jax.experimental import pallas as pl
from jax.experimental.pallas import tpu as pltpu
from jax.sharding import PartitionSpec as P

MASKED = -1e30
F32 = jnp.float32
BF16 = jnp.bfloat16
LANES = 128
RING = 4
USE = (0, 3, 2, 1)
ORDER = (3, 2, 1)


def ring_index(axis, stride):
    return lax.rem(lax.div(lax.axis_index(axis), stride), RING)


def partner(place, turn):
    return lax.bitwise_xor(place, turn)


def moved(part, axis, stride, turn):
    pairs = []
    for at in range(lax.axis_size(axis)):
        place = (at // stride) % RING
        pairs.append((at, at + ((place ^ turn) - place) * stride))
    return lax.ppermute(part, axis, pairs)


def exchanged(parts, axis, stride):
    received = {turn: moved(parts[turn], axis, stride, turn) for turn in ORDER}
    return [received.get(turn, parts[turn]) for turn in range(RING)]


def vmem(*arrays):
    return [pltpu.with_memory_space_constraint(array, pltpu.VMEM) for array in arrays]


def whole(count):
    return [pl.BlockSpec(memory_space=pltpu.VMEM)] * count


def kept(shape, dtype):
    return pltpu.VMEM(shape, dtype)


def params(mib):
    return pltpu.CompilerParams(vmem_limit_bytes=mib << 20)


def diagonal(size):
    rows = lax.broadcasted_iota(jnp.int32, (size, size), 0)
    columns = lax.broadcasted_iota(jnp.int32, (size, size), 1)
    return rows == columns


def three_parts(value):
    first = value.astype(BF16)
    rest = value - first.astype(F32)
    second = rest.astype(BF16)
    third = (rest - second.astype(F32)).astype(BF16)
    return first.astype(F32), second.astype(F32), third.astype(F32)


def packed_levels(level, rows):
    size = level.shape[0]
    line = jnp.sum(
        jnp.where(diagonal(size), jnp.broadcast_to(level, (size, size)), 0.0), axis=0, keepdims=True
    )
    row = lax.broadcasted_iota(jnp.int32, (rows, size), 0)
    tile = jnp.zeros((rows, size), F32)
    for at, part in enumerate(three_parts(line)):
        tile = jnp.where(row == at, jnp.broadcast_to(part, (rows, size)), tile)
    return tile.astype(BF16)


def attention_kernel(
    lengths_in,
    query_in,
    keys_in,
    values_in,
    fresh_keys_in,
    fresh_values_in,
    *refs,
):
    extra = (len(refs) - 8) // 2
    extras_in, out, extras = refs[:extra], refs[extra], refs[extra + 1 : 2 * extra + 1]
    lengths, query, keys, values, fresh_keys, fresh_values, sems = refs[2 * extra + 1 :]
    requests, rows, head_dim = query.shape
    slots = keys.shape[1]
    steps = fresh_keys.shape[1]
    moves = []
    for source, target in (
        (lengths_in, lengths),
        (query_in, query),
        (fresh_keys_in, fresh_keys),
        (keys_in, keys),
        (fresh_values_in, fresh_values),
        (values_in, values),
        *zip(extras_in, extras),
    ):
        moves.append(pltpu.make_async_copy(source, target, sems.at[len(moves)]))
        moves[-1].start()
    shard = lax.axis_index("kvseq")
    count = requests * rows
    fresh = requests * steps
    scale = 1.0 / math.sqrt(head_dim)
    contract = (((1,), (1,)), ((), ()))
    for move in moves[:4]:
        move.wait()
    fresh_row = lax.broadcasted_iota(jnp.int32, (count, fresh), 0)
    token = lax.broadcasted_iota(jnp.int32, (count, fresh), 1)
    per_step = rows // steps
    row_step = lax.div(fresh_row, per_step)
    same_request = lax.div(row_step, steps) == lax.div(token, steps)
    fresh_mask = same_request & (token <= jnp.where(shard == 0, row_step, -1))
    flat_keys = jnp.concatenate(
        [fresh_keys[request].astype(F32) for request in range(requests)], axis=0
    ).astype(BF16)
    everyone = jnp.concatenate([query[request] for request in range(requests)], axis=0)
    fresh_scores = jnp.where(
        fresh_mask,
        lax.dot_general(everyone, flat_keys, contract, preferred_element_type=F32) * scale,
        MASKED,
    )
    fresh_top = jnp.max(fresh_scores, axis=1, keepdims=True)
    slot = lax.broadcasted_iota(jnp.int32, (rows, slots), 1)
    tops, probs, totals = [], [], []
    for request in range(requests):
        mine = slice(request * rows, (request + 1) * rows)
        mask = slot < lengths[request] - shard * slots
        scores = jnp.where(
            mask,
            lax.dot_general(query[request], keys[request], contract, preferred_element_type=F32)
            * scale,
            MASKED,
        )
        top = jnp.maximum(jnp.max(scores, axis=1, keepdims=True), fresh_top[mine])
        prob = jnp.where(mask, jnp.exp(scores - top), 0.0)
        tops.append(top)
        totals.append(jnp.sum(prob, axis=1, keepdims=True))
        probs.append(prob.astype(BF16))
    top = jnp.concatenate(tops, axis=0)
    fresh_prob = jnp.where(fresh_mask, jnp.exp(fresh_scores - top), 0.0)
    total = jnp.concatenate(totals, axis=0) + jnp.sum(fresh_prob, axis=1, keepdims=True)
    for move in moves[4:6]:
        move.wait()
    flat_values = jnp.concatenate(
        [fresh_values[request].astype(F32) for request in range(requests)], axis=0
    ).astype(BF16)
    weighted = jnp.dot(fresh_prob.astype(BF16), flat_values, preferred_element_type=F32)
    weighted = weighted + jnp.concatenate(
        [
            jnp.dot(probs[request], values[request], preferred_element_type=F32)
            for request in range(requests)
        ],
        axis=0,
    )
    some = total > 0.0
    safe = jnp.where(some, total, 1.0)
    mean = weighted / safe
    level = jnp.where(some, top + jnp.log(safe), MASKED)
    half = rows // 2
    order = [
        slice(request * rows + part * half, request * rows + (part + 1) * half)
        for part in range(2)
        for request in range(requests)
    ]
    mean = jnp.concatenate([mean[rows_of] for rows_of in order], axis=0)
    level = jnp.concatenate([level[rows_of] for rows_of in order], axis=0)
    out[:count, :] = mean.astype(BF16)
    out[count:, :] = packed_levels(level, 16)
    for move in moves[6:]:
        move.wait()


def hbm(*arrays):
    return [pltpu.with_memory_space_constraint(array, pltpu.HBM) for array in arrays]


def anywhere(count):
    return [pl.BlockSpec(memory_space=pl.ANY)] * count


def attention(queries, new_keys, new_values, cache_keys, cache_values, lengths, extras):
    requests, slots, _, head_dim = cache_keys.shape
    rows = queries.shape[1] * queries.shape[2]
    steps = new_keys.shape[1]
    shapes = [
        (requests, rows, head_dim),
        (requests, slots, head_dim),
        (requests, slots, head_dim),
        (requests, steps, head_dim),
        (requests, steps, head_dim),
    ]
    arrays = (queries, cache_keys, cache_values, new_keys, new_values)
    return pl.pallas_call(
        attention_kernel,
        in_specs=anywhere(6 + len(extras)),
        out_specs=whole(1 + len(extras)),
        out_shape=(
            kept((requests * rows + 16, head_dim), BF16),
            *(kept(extra.shape, extra.dtype) for extra in extras),
        ),
        scratch_shapes=[
            pltpu.SMEM(lengths.shape, lengths.dtype),
            *(pltpu.VMEM(shape, BF16) for shape in shapes),
            pltpu.SemaphoreType.DMA((6 + len(extras),)),
        ],
        compiler_params=params(8),
        name="attention",
    )(
        *hbm(lengths, *(array.reshape(shape) for array, shape in zip(arrays, shapes)), *extras),
    )


def fetch_kernel(count, *refs):
    sources, targets, sems = refs[:count], refs[count + 1 : 2 * count + 1], refs[2 * count + 1]
    moves = []
    for source, target in zip(sources, targets):
        rows = source.shape[0]
        pieces = 4 if rows % 64 == 0 else 1
        for piece in range(pieces):
            part = pl.ds(piece * (rows // pieces), rows // pieces)
            moves.append(
                pltpu.make_async_copy(source.at[part], target.at[part], sems.at[len(moves)])
            )
            moves[-1].start()
    for move in moves:
        move.wait()


def fetched(arrays, after):
    count = len(arrays)
    moved_bytes = sum(array.size * array.dtype.itemsize for array in arrays)
    return pl.pallas_call(
        functools.partial(fetch_kernel, count),
        in_specs=anywhere(count + 1),
        out_specs=whole(count),
        out_shape=tuple(kept(array.shape, array.dtype) for array in arrays),
        scratch_shapes=[pltpu.SemaphoreType.DMA((4 * count,))],
        compiler_params=params(1),
        cost_estimate=pl.CostEstimate(flops=0, transcendentals=0, bytes_accessed=2 * moved_bytes),
        name="fetch",
    )(*hbm(*arrays), after)


def merge(parts):
    count = parts[0].shape[0] - 16
    same = diagonal(count)
    levels, means = [], []
    for part in parts:
        tail = part[count:, :].astype(F32)
        line = tail[0:1] + tail[1:2] + tail[2:3]
        levels.append(
            jnp.sum(
                jnp.where(same, jnp.broadcast_to(line, (count, count)), 0.0), axis=1, keepdims=True
            )
        )
        means.append(part[:count, :].astype(F32))
    top = functools.reduce(jnp.maximum, levels)
    scales = [jnp.exp(level - top) for level in levels]
    total = sum(scales)
    mean = sum(scale * mean for scale, mean in zip(scales, means)) / total
    return mean, top + jnp.log(total)


def merge_kernel(*refs):
    parts, out = refs[:RING], refs[RING + 1]
    mean, level = merge(parts)
    count = mean.shape[0]
    out[:count, :] = mean.astype(BF16)
    out[count:, :] = packed_levels(level, 16)


def merged(parts, after):
    return pl.pallas_call(
        merge_kernel,
        in_specs=whole(RING + 1),
        out_specs=whole(1)[0],
        out_shape=kept(parts[0].shape, BF16),
        compiler_params=params(4),
        name="merge_x",
    )(*vmem(*parts, after))


def project_kernel(*refs):
    parts, (weight, _, out, attended) = refs[:RING], refs[RING:]
    mean, _ = merge(parts)
    attended[...] = mean
    rows = out.shape[0]
    heads = mean.shape[0] // rows
    row = jnp.concatenate(
        [attended[pl.ds(head, rows, stride=heads), :].astype(BF16) for head in range(heads)], axis=1
    )
    out[...] = jnp.dot(row, weight[...], preferred_element_type=F32)


def projected(parts, weight, rows, after):
    count, head_dim = parts[0].shape
    return pl.pallas_call(
        project_kernel,
        in_specs=[*whole(RING + 1), *anywhere(1)],
        out_specs=whole(1)[0],
        out_shape=kept((rows, weight.shape[1]), F32),
        scratch_shapes=[pltpu.VMEM((count - 16, head_dim), F32)],
        compiler_params=params(4),
        name="merge_z_project",
    )(*vmem(*parts, weight, after))


def quarter_start(quarter, width, size):
    return pl.multiple_of(jnp.minimum(quarter * width, size - width), LANES)


def chunk_into(out, scaled, tail, gate, up, turn):
    width = (out.shape[1] - LANES) // 2
    quarter = partner(ring_index("kvseq", 1), turn)
    columns = pl.ds(quarter_start(quarter, width, gate.shape[1]), width)
    for offset, weight in ((0, gate), (width, up)):
        out[:, offset : offset + width] = jnp.dot(
            scaled, weight[:, columns], preferred_element_type=F32
        ).astype(BF16)
    out[:, 2 * width :] = tail


def pair_kernel(mine, other, pair, half):
    total = (mine[...] + other[...]).astype(BF16)
    pair[...] = total
    width = half.shape[1]
    core = lax.rem(lax.axis_index("kvhead"), 2)
    half[...] = jnp.where(core == 0, total[:, :width], total[:, width:])


def join_kernel(whole_part, half_part, _, out):
    half = half_part[...].astype(F32)
    none = jnp.zeros_like(half)
    core = lax.rem(lax.axis_index("kvhead"), 2)
    left, right = jnp.where(core == 0, half, none), jnp.where(core == 0, none, half)
    out[...] = whole_part[...].astype(F32) + jnp.concatenate([left, right], axis=1)


def pair_of(mine, other):
    rows, columns = mine.shape
    return pl.pallas_call(
        pair_kernel,
        in_specs=whole(2),
        out_specs=whole(2),
        out_shape=(kept((rows, columns), BF16), kept((rows, columns // 2), BF16)),
        compiler_params=params(1),
        name="pair",
    )(*vmem(mine, other))


def from_chips(pair, half, after):
    size = lax.axis_size("kvhead")
    split = [(at, at ^ (2 if at % 2 == 0 else 6)) for at in range(size)]
    return pl.pallas_call(
        join_kernel,
        in_specs=[*whole(2), *anywhere(1)],
        out_specs=whole(1)[0],
        out_shape=kept(pair.shape, F32),
        compiler_params=params(1),
        name="join",
    )(*vmem(lax.ppermute(pair, "kvhead", split), moved(half, "kvhead", 2, 2), after))


def first_up_kernel(hidden_in, *refs):
    parts, (gain, gate, up, *refs) = refs[:3], refs[3:]
    outs, (residual, scaled, tail) = refs[: RING - 1], refs[RING - 1 :]
    before = hidden_in[...].astype(F32)
    pair = before.shape[0] // (2 * RING)
    before = jnp.concatenate(
        [
            before[(2 * request + part) * pair : (2 * request + part + 1) * pair]
            for part in range(2)
            for request in range(RING)
        ],
        axis=0,
    )
    total = before + sum(part[...].astype(F32) for part in parts)
    residual[...] = total
    squares = jnp.sum(total * total, axis=1, keepdims=True)
    high = squares.astype(BF16).astype(F32)
    lane = lax.broadcasted_iota(jnp.int32, (total.shape[0], LANES), 1)
    tail[...] = jnp.where(lane < LANES // 2, high, squares - high).astype(BF16)
    scaled[...] = (total * gain[...]).astype(BF16)
    for turn, out in enumerate(outs, 1):
        chunk_into(out, scaled[...], tail[...], gate, up, turn)


def own_up_kernel(scaled, tail, gate, up, out):
    chunk_into(out, scaled[...], tail[...], gate, up, 0)


def up_projected(hidden_in, parts, gain, gate, up, width):
    rows, depth = hidden_in.shape
    chunk = kept((rows, 2 * width + LANES), BF16)
    *chunks, residual, scaled, tail = pl.pallas_call(
        first_up_kernel,
        in_specs=whole(7),
        out_specs=whole(RING + 2),
        out_shape=(
            *[chunk] * (RING - 1),
            kept((rows, depth), F32),
            kept((rows, depth), BF16),
            kept((rows, LANES), BF16),
        ),
        compiler_params=params(4),
        name="gate_up_others",
    )(*vmem(hidden_in, *parts, gain, gate, up))
    own = pl.pallas_call(
        own_up_kernel,
        in_specs=whole(4),
        out_specs=whole(1)[0],
        out_shape=chunk,
        compiler_params=params(4),
        name="gate_up_own",
    )(*vmem(scaled, tail, gate, up))
    return [own, *chunks], residual


def summed(parts, width):
    total = sum(part[:, : 2 * width].astype(F32) for part in parts)
    tail = sum(part[:, 2 * width :].astype(F32) for part in parts)
    return total, tail


def sum_kernel(width, *refs):
    total, tail = summed(refs[:RING], width)
    out = refs[RING]
    out[:, : 2 * width] = total.astype(BF16)
    high = tail.astype(BF16)
    out[:, 2 * width : 2 * width + LANES] = high
    out[:, 2 * width + LANES :] = (tail - high.astype(F32)).astype(BF16)


def summed_terms(parts, width):
    return pl.pallas_call(
        functools.partial(sum_kernel, width),
        in_specs=whole(RING),
        out_specs=whole(1)[0],
        out_shape=kept((parts[0].shape[0], 2 * (width + LANES)), BF16),
        compiler_params=params(4),
        name="sum_x",
    )(*vmem(*parts))


def hidden_kernel(width, full_width, units, *refs):
    total, tail = summed(refs[:RING], width)
    out = refs[RING]
    tail = tail[:, :LANES] + tail[:, LANES:]
    squares = tail[:, :1] + tail[:, LANES // 2 : LANES // 2 + 1]
    scale = 1.0 / jnp.sqrt(squares / full_width + 1e-05)
    gate_total = total[:, :width] * scale
    up_total = total[:, width:] * scale
    hidden = gate_total / (1.0 + jnp.exp(-gate_total)) * up_total
    quarter = ring_index("kvseq", 1)
    twice = quarter * width - quarter_start(quarter, width, units)
    lane = lax.broadcasted_iota(jnp.int32, hidden.shape, 1)
    out[...] = jnp.where(lane < twice, 0.0, hidden).astype(BF16)


def hidden_units(parts, width, full_width, units):
    return pl.pallas_call(
        functools.partial(hidden_kernel, width, full_width, units),
        in_specs=whole(RING),
        out_specs=whole(1)[0],
        out_shape=kept((parts[0].shape[0], width), BF16),
        compiler_params=params(4),
        name="sum_z_hidden",
    )(*vmem(*parts))


def down_term(hidden, weight, turn):
    width = hidden.shape[1]
    quarter = partner(ring_index("kvseq", 1), turn)
    rows = pl.ds(quarter_start(quarter, width, weight.shape[0]), width)
    return jnp.dot(hidden[...], weight[rows, :], preferred_element_type=F32)


def first_down_kernel(hidden, weight, out):
    out[...] = down_term(hidden, weight, 0)


def next_down_kernel(turn, before, hidden, weight, out):
    out[...] = before[...] + down_term(hidden, weight, turn)


def last_down_kernel(turn, before, hidden, weight, own, other, terms):
    core = lax.rem(lax.axis_index("kvhead"), 2)
    terms[...] = before[...] + down_term(hidden, weight, turn)
    half = own.shape[0]
    own[...] = terms[pl.ds(pl.multiple_of(core * half, half), half), :]
    other[...] = terms[pl.ds(pl.multiple_of((1 - core) * half, half), half), :]


def down_projected(parts, weight):
    rows, columns = parts[0].shape[0], weight.shape[1]
    full, half = kept((rows, columns), F32), kept((rows // 2, columns), F32)
    terms = pl.pallas_call(
        first_down_kernel,
        in_specs=whole(2),
        out_specs=whole(1)[0],
        out_shape=full,
        compiler_params=params(4),
        name="down_0",
    )(*vmem(parts[0], weight))
    for turn in ORDER[:-1]:
        terms = pl.pallas_call(
            functools.partial(next_down_kernel, turn),
            in_specs=whole(3),
            out_specs=whole(1)[0],
            out_shape=full,
            compiler_params=params(4),
            name=f"down_{turn}",
        )(*vmem(terms, parts[turn], weight))
    return pl.pallas_call(
        functools.partial(last_down_kernel, ORDER[-1]),
        in_specs=whole(3),
        out_specs=whole(2),
        out_shape=(half, half),
        scratch_shapes=[pltpu.VMEM((rows, columns), F32)],
        compiler_params=params(4),
        name="down_last",
    )(*vmem(terms, parts[ORDER[-1]], weight))


def rows_kernel(own, other, residual, *refs):
    outs, held = refs[:RING], refs[RING]
    place = ring_index("kvhead", 2)
    core = lax.rem(lax.axis_index("kvhead"), 2)
    half = own.shape[0]
    mine = residual[pl.ds(pl.multiple_of(core * half, half), half), :]
    total = own[...] + other[...]
    each = half // RING
    for part in range(RING):
        rows = slice(part * each, (part + 1) * each)
        held[part] = total[rows] + jnp.where(part == place, mine[rows], 0.0)
    for turn in range(RING):
        outs[turn][...] = held[partner(place, turn)]


def row_chunks(own, other, residual):
    half, columns = own.shape
    each = half // RING
    return pl.pallas_call(
        rows_kernel,
        in_specs=whole(3),
        out_specs=whole(RING),
        out_shape=(kept((each, columns), F32),) * RING,
        scratch_shapes=[pltpu.VMEM((RING, each, columns), F32)],
        compiler_params=params(4),
        name="row_chunks",
    )(*vmem(own, other, residual))


def row_sum_kernel(first, second, third, fourth, out):
    out[...] = (first[...] + second[...] + third[...] + fourth[...]).astype(BF16)


def row_sum(parts):
    return pl.pallas_call(
        row_sum_kernel,
        in_specs=whole(RING),
        out_specs=whole(1)[0],
        out_shape=jax.ShapeDtypeStruct(parts[0].shape, BF16),
        compiler_params=params(1),
        name="row_sum",
    )(*vmem(*parts))


def swapped(part):
    size = lax.axis_size("kvhead")
    return lax.ppermute(part, "kvhead", [(at, at ^ 1) for at in range(size)])


def local(
    hidden_in,
    queries,
    new_keys,
    new_values,
    cache_keys,
    cache_values,
    lengths,
    out_weight,
    norm_gain,
    gate_weight,
    up_weight,
    down_weight,
):
    requests, steps = queries.shape[:2]
    rows = requests * steps
    depth = hidden_in.shape[1]
    full_width = depth * lax.axis_size("kvseq")
    units = gate_weight.shape[1]
    width = -(-units // (RING * LANES)) * LANES
    part, out_held, hidden_held = attention(
        queries,
        new_keys,
        new_values,
        cache_keys,
        cache_values,
        lengths,
        [out_weight, hidden_in],
    )
    gate_held, gain_held = fetched([gate_weight, norm_gain.reshape(1, depth)], part)
    part = merged(exchanged([part] * RING, "kvseq", 1), gain_held)
    (up_held,) = fetched([up_weight], part)
    terms = projected(exchanged([part] * RING, "kvseq", RING), out_held, rows, up_held)
    pair, half = pair_of(terms, swapped(terms))
    (down_held,) = fetched([down_weight], pair)
    got = from_chips(pair, half, down_held)
    chunks, residual = up_projected(
        hidden_held, [pair, got, swapped(got)], gain_held, gate_held, up_held, width
    )
    received = exchanged(chunks, "kvseq", 1)
    total = summed_terms([received[turn] for turn in USE], width)
    hidden = hidden_units(exchanged([total] * RING, "kvseq", RING), width, full_width, units)
    own, other = down_projected(exchanged([hidden] * RING, "kvseq", 1), down_held)
    shares = exchanged(row_chunks(own, swapped(other), residual), "kvhead", 2)
    return row_sum([shares[turn] for turn in USE])


def solution(mesh):
    in_specs = (
        P(None, "kvseq"),
        P(None, None, "kvhead", None),
        P(None, None, "kvhead", None),
        P(None, None, "kvhead", None),
        P(None, "kvseq", "kvhead", None),
        P(None, "kvseq", "kvhead", None),
        P(),
        P("kvhead", "kvseq"),
        P("kvseq"),
        P("kvseq", "kvhead"),
        P("kvseq", "kvhead"),
        P("kvhead", "kvseq"),
    )
    out_specs = P("kvhead", "kvseq")
    return jax.shard_map(local, mesh=mesh, in_specs=in_specs, out_specs=out_specs, check_vma=False)
```

```python
import functools
import math

import jax
import jax.numpy as jnp
from jax import lax
from jax.experimental import pallas as pl
from jax.experimental.pallas import tpu as pltpu
from jax.sharding import PartitionSpec as P

MASKED = -1e30
F32 = jnp.float32
BF16 = jnp.bfloat16
LANES = 128
RING = 4
USE = (0, 3, 2, 1)
ORDER = (3, 2, 1)


def ring_index(axis, stride):
    return lax.rem(lax.div(lax.axis_index(axis), stride), RING)


def partner(place, turn):
    return lax.bitwise_xor(place, turn)


def moved(part, axis, stride, turn):
    pairs = []
    for at in range(lax.axis_size(axis)):
        place = (at // stride) % RING
        pairs.append((at, at + ((place ^ turn) - place) * stride))
    return lax.ppermute(part, axis, pairs)


def exchanged(parts, axis, stride):
    received = {turn: moved(parts[turn], axis, stride, turn) for turn in ORDER}
    return [received.get(turn, parts[turn]) for turn in range(RING)]


def vmem(*arrays):
    return [pltpu.with_memory_space_constraint(array, pltpu.VMEM) for array in arrays]


def whole(count):
    return [pl.BlockSpec(memory_space=pltpu.VMEM)] * count


def kept(shape, dtype):
    return pltpu.VMEM(shape, dtype)


def params(mib):
    return pltpu.CompilerParams(vmem_limit_bytes=mib << 20)


def diagonal(size):
    rows = lax.broadcasted_iota(jnp.int32, (size, size), 0)
    columns = lax.broadcasted_iota(jnp.int32, (size, size), 1)
    return rows == columns


def three_parts(value):
    first = value.astype(BF16)
    rest = value - first.astype(F32)
    second = rest.astype(BF16)
    third = (rest - second.astype(F32)).astype(BF16)
    return first.astype(F32), second.astype(F32), third.astype(F32)


def packed_levels(level, rows):
    size = level.shape[0]
    line = jnp.sum(
        jnp.where(diagonal(size), jnp.broadcast_to(level, (size, size)), 0.0), axis=0, keepdims=True
    )
    row = lax.broadcasted_iota(jnp.int32, (rows, size), 0)
    tile = jnp.zeros((rows, size), F32)
    for at, part in enumerate(three_parts(line)):
        tile = jnp.where(row == at, jnp.broadcast_to(part, (rows, size)), tile)
    return tile.astype(BF16)


def attention_kernel(
    lengths_in,
    query_in,
    keys_in,
    values_in,
    fresh_keys_in,
    fresh_values_in,
    *refs,
):
    extra = (len(refs) - 8) // 2
    extras_in, out, extras = refs[:extra], refs[extra], refs[extra + 1 : 2 * extra + 1]
    lengths, query, keys, values, fresh_keys, fresh_values, sems = refs[2 * extra + 1 :]
    requests, rows, head_dim = query.shape
    slots = keys.shape[1]
    steps = fresh_keys.shape[1]
    moves = []
    for source, target in (
        (lengths_in, lengths),
        (query_in, query),
        (fresh_keys_in, fresh_keys),
        (keys_in, keys),
        (fresh_values_in, fresh_values),
        (values_in, values),
        *zip(extras_in, extras),
    ):
        moves.append(pltpu.make_async_copy(source, target, sems.at[len(moves)]))
        moves[-1].start()
    shard = lax.axis_index("kvseq")
    count = requests * rows
    fresh = requests * steps
    scale = 1.0 / math.sqrt(head_dim)
    contract = (((1,), (1,)), ((), ()))
    for move in moves[:4]:
        move.wait()
    fresh_row = lax.broadcasted_iota(jnp.int32, (count, fresh), 0)
    token = lax.broadcasted_iota(jnp.int32, (count, fresh), 1)
    per_step = rows // steps
    row_step = lax.div(fresh_row, per_step)
    same_request = lax.div(row_step, steps) == lax.div(token, steps)
    fresh_mask = same_request & (token <= jnp.where(shard == 0, row_step, -1))
    flat_keys = jnp.concatenate(
        [fresh_keys[request].astype(F32) for request in range(requests)], axis=0
    ).astype(BF16)
    everyone = jnp.concatenate([query[request] for request in range(requests)], axis=0)
    fresh_scores = jnp.where(
        fresh_mask,
        lax.dot_general(everyone, flat_keys, contract, preferred_element_type=F32) * scale,
        MASKED,
    )
    fresh_top = jnp.max(fresh_scores, axis=1, keepdims=True)
    slot = lax.broadcasted_iota(jnp.int32, (rows, slots), 1)
    tops, probs, totals = [], [], []
    for request in range(requests):
        mine = slice(request * rows, (request + 1) * rows)
        mask = slot < lengths[request] - shard * slots
        scores = jnp.where(
            mask,
            lax.dot_general(query[request], keys[request], contract, preferred_element_type=F32)
            * scale,
            MASKED,
        )
        top = jnp.maximum(jnp.max(scores, axis=1, keepdims=True), fresh_top[mine])
        prob = jnp.where(mask, jnp.exp(scores - top), 0.0)
        tops.append(top)
        totals.append(jnp.sum(prob, axis=1, keepdims=True))
        probs.append(prob.astype(BF16))
    top = jnp.concatenate(tops, axis=0)
    fresh_prob = jnp.where(fresh_mask, jnp.exp(fresh_scores - top), 0.0)
    total = jnp.concatenate(totals, axis=0) + jnp.sum(fresh_prob, axis=1, keepdims=True)
    for move in moves[4:6]:
        move.wait()
    flat_values = jnp.concatenate(
        [fresh_values[request].astype(F32) for request in range(requests)], axis=0
    ).astype(BF16)
    weighted = jnp.dot(fresh_prob.astype(BF16), flat_values, preferred_element_type=F32)
    weighted = weighted + jnp.concatenate(
        [
            jnp.dot(probs[request], values[request], preferred_element_type=F32)
            for request in range(requests)
        ],
        axis=0,
    )
    some = total > 0.0
    safe = jnp.where(some, total, 1.0)
    mean = weighted / safe
    level = jnp.where(some, top + jnp.log(safe), MASKED)
    half = rows // 2
    order = [
        slice(request * rows + part * half, request * rows + (part + 1) * half)
        for part in range(2)
        for request in range(requests)
    ]
    mean = jnp.concatenate([mean[rows_of] for rows_of in order], axis=0)
    level = jnp.concatenate([level[rows_of] for rows_of in order], axis=0)
    out[:count, :] = mean.astype(BF16)
    out[count:, :] = packed_levels(level, 16)
    for move in moves[6:]:
        move.wait()


def hbm(*arrays):
    return [pltpu.with_memory_space_constraint(array, pltpu.HBM) for array in arrays]


def anywhere(count):
    return [pl.BlockSpec(memory_space=pl.ANY)] * count


def attention(queries, new_keys, new_values, cache_keys, cache_values, lengths, extras):
    requests, slots, _, head_dim = cache_keys.shape
    rows = queries.shape[1] * queries.shape[2]
    steps = new_keys.shape[1]
    shapes = [
        (requests, rows, head_dim),
        (requests, slots, head_dim),
        (requests, slots, head_dim),
        (requests, steps, head_dim),
        (requests, steps, head_dim),
    ]
    arrays = (queries, cache_keys, cache_values, new_keys, new_values)
    return pl.pallas_call(
        attention_kernel,
        in_specs=anywhere(6 + len(extras)),
        out_specs=whole(1 + len(extras)),
        out_shape=(
            kept((requests * rows + 16, head_dim), BF16),
            *(kept(extra.shape, extra.dtype) for extra in extras),
        ),
        scratch_shapes=[
            pltpu.SMEM(lengths.shape, lengths.dtype),
            *(pltpu.VMEM(shape, BF16) for shape in shapes),
            pltpu.SemaphoreType.DMA((6 + len(extras),)),
        ],
        compiler_params=params(8),
        name="attention",
    )(
        *hbm(lengths, *(array.reshape(shape) for array, shape in zip(arrays, shapes)), *extras),
    )


def fetch_kernel(count, *refs):
    sources, targets, sems = refs[:count], refs[count + 1 : 2 * count + 1], refs[2 * count + 1]
    moves = []
    for source, target in zip(sources, targets):
        rows = source.shape[0]
        pieces = 4 if rows % 64 == 0 else 1
        for piece in range(pieces):
            part = pl.ds(piece * (rows // pieces), rows // pieces)
            moves.append(
                pltpu.make_async_copy(source.at[part], target.at[part], sems.at[len(moves)])
            )
            moves[-1].start()
    for move in moves:
        move.wait()


def fetched(arrays, after):
    count = len(arrays)
    moved_bytes = sum(array.size * array.dtype.itemsize for array in arrays)
    return pl.pallas_call(
        functools.partial(fetch_kernel, count),
        in_specs=anywhere(count + 1),
        out_specs=whole(count),
        out_shape=tuple(kept(array.shape, array.dtype) for array in arrays),
        scratch_shapes=[pltpu.SemaphoreType.DMA((4 * count,))],
        compiler_params=params(1),
        cost_estimate=pl.CostEstimate(flops=0, transcendentals=0, bytes_accessed=2 * moved_bytes),
        name="fetch",
    )(*hbm(*arrays), after)


def merge(parts):
    count = parts[0].shape[0] - 16
    same = diagonal(count)
    levels, means = [], []
    for part in parts:
        tail = part[count:, :].astype(F32)
        line = tail[0:1] + tail[1:2] + tail[2:3]
        levels.append(
            jnp.sum(
                jnp.where(same, jnp.broadcast_to(line, (count, count)), 0.0), axis=1, keepdims=True
            )
        )
        means.append(part[:count, :].astype(F32))
    top = functools.reduce(jnp.maximum, levels)
    scales = [jnp.exp(level - top) for level in levels]
    total = sum(scales)
    mean = sum(scale * mean for scale, mean in zip(scales, means)) / total
    return mean, top + jnp.log(total)


def merge_kernel(*refs):
    parts, out = refs[:RING], refs[RING + 1]
    mean, level = merge(parts)
    count = mean.shape[0]
    out[:count, :] = mean.astype(BF16)
    out[count:, :] = packed_levels(level, 16)


def merged(parts, after):
    return pl.pallas_call(
        merge_kernel,
        in_specs=whole(RING + 1),
        out_specs=whole(1)[0],
        out_shape=kept(parts[0].shape, BF16),
        compiler_params=params(4),
        name="merge_x",
    )(*vmem(*parts, after))


def project_kernel(*refs):
    parts, (weight, _, out, attended) = refs[:RING], refs[RING:]
    mean, _ = merge(parts)
    attended[...] = mean
    rows = out.shape[0]
    heads = mean.shape[0] // rows
    row = jnp.concatenate(
        [attended[pl.ds(head, rows, stride=heads), :].astype(BF16) for head in range(heads)], axis=1
    )
    out[...] = jnp.dot(row, weight[...], preferred_element_type=F32)


def projected(parts, weight, rows, after):
    count, head_dim = parts[0].shape
    return pl.pallas_call(
        project_kernel,
        in_specs=[*whole(RING + 1), *anywhere(1)],
        out_specs=whole(1)[0],
        out_shape=kept((rows, weight.shape[1]), F32),
        scratch_shapes=[pltpu.VMEM((count - 16, head_dim), F32)],
        compiler_params=params(4),
        name="merge_z_project",
    )(*vmem(*parts, weight, after))


def quarter_start(quarter, width, size):
    return pl.multiple_of(jnp.minimum(quarter * width, size - width), LANES)


def chunk_into(out, scaled, tail, gate, up, turn):
    width = (out.shape[1] - LANES) // 2
    quarter = partner(ring_index("kvseq", 1), turn)
    columns = pl.ds(quarter_start(quarter, width, gate.shape[1]), width)
    for offset, weight in ((0, gate), (width, up)):
        out[:, offset : offset + width] = jnp.dot(
            scaled, weight[:, columns], preferred_element_type=F32
        ).astype(BF16)
    out[:, 2 * width :] = tail


def pair_kernel(mine, other, pair, half):
    total = (mine[...] + other[...]).astype(BF16)
    pair[...] = total
    width = half.shape[1]
    core = lax.rem(lax.axis_index("kvhead"), 2)
    half[...] = jnp.where(core == 0, total[:, :width], total[:, width:])


def join_kernel(whole_part, half_part, out):
    half = half_part[...].astype(F32)
    none = jnp.zeros_like(half)
    core = lax.rem(lax.axis_index("kvhead"), 2)
    left, right = jnp.where(core == 0, half, none), jnp.where(core == 0, none, half)
    out[...] = whole_part[...].astype(F32) + jnp.concatenate([left, right], axis=1)


def pair_of(mine, other):
    rows, columns = mine.shape
    return pl.pallas_call(
        pair_kernel,
        in_specs=whole(2),
        out_specs=whole(2),
        out_shape=(kept((rows, columns), BF16), kept((rows, columns // 2), BF16)),
        compiler_params=params(1),
        name="pair",
    )(*vmem(mine, other))


def from_chips(pair, half):
    size = lax.axis_size("kvhead")
    split = [(at, at ^ (2 if at % 2 == 0 else 6)) for at in range(size)]
    return pl.pallas_call(
        join_kernel,
        in_specs=whole(2),
        out_specs=whole(1)[0],
        out_shape=kept(pair.shape, F32),
        compiler_params=params(1),
        name="join",
    )(*vmem(lax.ppermute(pair, "kvhead", split), moved(half, "kvhead", 2, 2)))


def first_up_kernel(hidden_in, *refs):
    parts, (gain, gate, up, *refs) = refs[:3], refs[3:]
    outs, (residual, scaled, tail) = refs[: RING - 1], refs[RING - 1 :]
    before = hidden_in[...].astype(F32)
    pair = before.shape[0] // (2 * RING)
    before = jnp.concatenate(
        [
            before[(2 * request + part) * pair : (2 * request + part + 1) * pair]
            for part in range(2)
            for request in range(RING)
        ],
        axis=0,
    )
    total = before + sum(part[...].astype(F32) for part in parts)
    residual[...] = total
    squares = jnp.sum(total * total, axis=1, keepdims=True)
    high = squares.astype(BF16).astype(F32)
    lane = lax.broadcasted_iota(jnp.int32, (total.shape[0], LANES), 1)
    tail[...] = jnp.where(lane < LANES // 2, high, squares - high).astype(BF16)
    scaled[...] = (total * gain[...]).astype(BF16)
    for turn, out in enumerate(outs, 1):
        chunk_into(out, scaled[...], tail[...], gate, up, turn)


def own_up_kernel(scaled, tail, gate, up, out):
    chunk_into(out, scaled[...], tail[...], gate, up, 0)


def up_projected(hidden_in, parts, gain, gate, up, width):
    rows, depth = hidden_in.shape
    chunk = kept((rows, 2 * width + LANES), BF16)
    *chunks, residual, scaled, tail = pl.pallas_call(
        first_up_kernel,
        in_specs=whole(7),
        out_specs=whole(RING + 2),
        out_shape=(
            *[chunk] * (RING - 1),
            kept((rows, depth), F32),
            kept((rows, depth), BF16),
            kept((rows, LANES), BF16),
        ),
        compiler_params=params(4),
        name="gate_up_others",
    )(*vmem(hidden_in, *parts, gain, gate, up))
    own = pl.pallas_call(
        own_up_kernel,
        in_specs=whole(4),
        out_specs=whole(1)[0],
        out_shape=chunk,
        compiler_params=params(4),
        name="gate_up_own",
    )(*vmem(scaled, tail, gate, up))
    return [own, *chunks], residual


def summed(parts, width):
    total = sum(part[:, : 2 * width].astype(F32) for part in parts)
    tail = sum(part[:, 2 * width :].astype(F32) for part in parts)
    return total, tail


def sum_kernel(width, *refs):
    total, tail = summed(refs[:RING], width)
    out = refs[RING]
    out[:, : 2 * width] = total.astype(BF16)
    high = tail.astype(BF16)
    out[:, 2 * width : 2 * width + LANES] = high
    out[:, 2 * width + LANES :] = (tail - high.astype(F32)).astype(BF16)


def summed_terms(parts, width):
    return pl.pallas_call(
        functools.partial(sum_kernel, width),
        in_specs=whole(RING),
        out_specs=whole(1)[0],
        out_shape=kept((parts[0].shape[0], 2 * (width + LANES)), BF16),
        compiler_params=params(4),
        name="sum_x",
    )(*vmem(*parts))


def hidden_kernel(width, full_width, units, *refs):
    total, tail = summed(refs[:RING], width)
    out = refs[RING + 1]
    tail = tail[:, :LANES] + tail[:, LANES:]
    squares = tail[:, :1] + tail[:, LANES // 2 : LANES // 2 + 1]
    scale = 1.0 / jnp.sqrt(squares / full_width + 1e-05)
    gate_total = total[:, :width] * scale
    up_total = total[:, width:] * scale
    hidden = gate_total / (1.0 + jnp.exp(-gate_total)) * up_total
    quarter = ring_index("kvseq", 1)
    twice = quarter * width - quarter_start(quarter, width, units)
    lane = lax.broadcasted_iota(jnp.int32, hidden.shape, 1)
    out[...] = jnp.where(lane < twice, 0.0, hidden).astype(BF16)


def hidden_units(parts, width, full_width, units, after):
    return pl.pallas_call(
        functools.partial(hidden_kernel, width, full_width, units),
        in_specs=[*whole(RING), *anywhere(1)],
        out_specs=whole(1)[0],
        out_shape=kept((parts[0].shape[0], width), BF16),
        compiler_params=params(4),
        name="sum_z_hidden",
    )(*vmem(*parts, after))


def down_term(hidden, weight, turn):
    width = hidden.shape[1]
    quarter = partner(ring_index("kvseq", 1), turn)
    rows = pl.ds(quarter_start(quarter, width, weight.shape[0]), width)
    return jnp.dot(hidden[...], weight[rows, :], preferred_element_type=F32)


def first_down_kernel(hidden, weight, out):
    out[...] = down_term(hidden, weight, 0)


def next_down_kernel(turn, before, hidden, weight, out):
    out[...] = before[...] + down_term(hidden, weight, turn)


def last_down_kernel(turn, before, hidden, weight, own, other, terms):
    core = lax.rem(lax.axis_index("kvhead"), 2)
    terms[...] = before[...] + down_term(hidden, weight, turn)
    half = own.shape[0]
    own[...] = terms[pl.ds(pl.multiple_of(core * half, half), half), :]
    other[...] = terms[pl.ds(pl.multiple_of((1 - core) * half, half), half), :]


def down_projected(parts, weight):
    rows, columns = parts[0].shape[0], weight.shape[1]
    full, half = kept((rows, columns), F32), kept((rows // 2, columns), F32)
    terms = pl.pallas_call(
        first_down_kernel,
        in_specs=whole(2),
        out_specs=whole(1)[0],
        out_shape=full,
        compiler_params=params(4),
        name="down_0",
    )(*vmem(parts[0], weight))
    for turn in ORDER[:-1]:
        terms = pl.pallas_call(
            functools.partial(next_down_kernel, turn),
            in_specs=whole(3),
            out_specs=whole(1)[0],
            out_shape=full,
            compiler_params=params(4),
            name=f"down_{turn}",
        )(*vmem(terms, parts[turn], weight))
    return pl.pallas_call(
        functools.partial(last_down_kernel, ORDER[-1]),
        in_specs=whole(3),
        out_specs=whole(2),
        out_shape=(half, half),
        scratch_shapes=[pltpu.VMEM((rows, columns), F32)],
        compiler_params=params(4),
        name="down_last",
    )(*vmem(terms, parts[ORDER[-1]], weight))


def rows_kernel(own, other, residual, *refs):
    outs, held = refs[:RING], refs[RING]
    place = ring_index("kvhead", 2)
    core = lax.rem(lax.axis_index("kvhead"), 2)
    half = own.shape[0]
    mine = residual[pl.ds(pl.multiple_of(core * half, half), half), :]
    total = own[...] + other[...]
    each = half // RING
    for part in range(RING):
        rows = slice(part * each, (part + 1) * each)
        held[part] = total[rows] + jnp.where(part == place, mine[rows], 0.0)
    for turn in range(RING):
        outs[turn][...] = held[partner(place, turn)]


def row_chunks(own, other, residual):
    half, columns = own.shape
    each = half // RING
    return pl.pallas_call(
        rows_kernel,
        in_specs=whole(3),
        out_specs=whole(RING),
        out_shape=(kept((each, columns), F32),) * RING,
        scratch_shapes=[pltpu.VMEM((RING, each, columns), F32)],
        compiler_params=params(4),
        name="row_chunks",
    )(*vmem(own, other, residual))


def row_sum_kernel(first, second, third, fourth, out):
    out[...] = (first[...] + second[...] + third[...] + fourth[...]).astype(BF16)


def row_sum(parts):
    return pl.pallas_call(
        row_sum_kernel,
        in_specs=whole(RING),
        out_specs=whole(1)[0],
        out_shape=jax.ShapeDtypeStruct(parts[0].shape, BF16),
        compiler_params=params(1),
        name="row_sum",
    )(*vmem(*parts))


def swapped(part):
    size = lax.axis_size("kvhead")
    return lax.ppermute(part, "kvhead", [(at, at ^ 1) for at in range(size)])


def local(
    hidden_in,
    queries,
    new_keys,
    new_values,
    cache_keys,
    cache_values,
    lengths,
    out_weight,
    norm_gain,
    gate_weight,
    up_weight,
    down_weight,
):
    requests, steps = queries.shape[:2]
    rows = requests * steps
    depth = hidden_in.shape[1]
    full_width = depth * lax.axis_size("kvseq")
    units = gate_weight.shape[1]
    width = -(-units // (RING * LANES)) * LANES
    part, out_held, hidden_held = attention(
        queries,
        new_keys,
        new_values,
        cache_keys,
        cache_values,
        lengths,
        [out_weight, hidden_in],
    )
    gate_held, gain_held = fetched([gate_weight, norm_gain.reshape(1, depth)], part)
    part = merged(exchanged([part] * RING, "kvseq", 1), gain_held)
    (up_held,) = fetched([up_weight], part)
    terms = projected(exchanged([part] * RING, "kvseq", RING), out_held, rows, up_held)
    pair, half = pair_of(terms, swapped(terms))
    got = from_chips(pair, half)
    chunks, residual = up_projected(
        hidden_held, [pair, got, swapped(got)], gain_held, gate_held, up_held, width
    )
    received = exchanged(chunks, "kvseq", 1)
    total = summed_terms([received[turn] for turn in USE], width)
    (down_held,) = fetched([down_weight], total)
    hidden = hidden_units(exchanged([total] * RING, "kvseq", RING), width, full_width, units, down_held)
    own, other = down_projected(exchanged([hidden] * RING, "kvseq", 1), down_held)
    shares = exchanged(row_chunks(own, swapped(other), residual), "kvhead", 2)
    return row_sum([shares[turn] for turn in USE])


def solution(mesh):
    in_specs = (
        P(None, "kvseq"),
        P(None, None, "kvhead", None),
        P(None, None, "kvhead", None),
        P(None, None, "kvhead", None),
        P(None, "kvseq", "kvhead", None),
        P(None, "kvseq", "kvhead", None),
        P(),
        P("kvhead", "kvseq"),
        P("kvseq"),
        P("kvseq", "kvhead"),
        P("kvseq", "kvhead"),
        P("kvhead", "kvseq"),
    )
    out_specs = P("kvhead", "kvseq")
    return jax.shard_map(local, mesh=mesh, in_specs=in_specs, out_specs=out_specs, check_vma=False)
```
